512 devices in a mesh: gx: 32 (over z, x), gy: 16 (over y, core).
Axes of the slice: x: 4, y: 8, z: 8, core: 2. Of those that a mesh axis runs over, the one named last changes fastest.
Arguments:
- fields: bfloat16 [4, 256, 512, 256], P(None, 'gx', 'gy'), may hold values from -6 to 6
- rows_live: int32 [32], replicated, may hold values from 4 to 8, as said below
- cols_live: int32 [16], replicated, may hold values from 16 to 32, as said below
- weight: bfloat16 [32, 108], replicated, may hold values from -0.625 to 0.625
- bias: float32 [32], replicated, may hold values from -3 to 3
- grad_out: bfloat16 [32, 128, 256, 128], P('gy', 'gx'), may hold values from -0.0234375 to 0.0234375
Outputs:
- stem: bfloat16 [32, 128, 256, 128], P('gy', 'gx')
- weight_grad: float32 [32, 108], P('gy')
- bias_grad: float32 [32], P('gy')
The draws below stay inside these ranges and needn't reach their ends.
Inputs may be any that keep to these rules, and one draw needn't show every extreme that they name: `rows_live`: every entry is even, and some entry equals 8. `cols_live`: every entry is even, and some entry equals 32.
All inputs are finite; a program needn't handle non-finite values.
Results may differ from the reference program's by a relative error of at most 0.0054.
Values may be sent and summed in bfloat16 or wider, within the bound.
A program may use at most 64 MiB of HBM per device.

```python
import jax
import jax.numpy as jnp
from jax import lax

CIN = 4
COUT = 32
CAPX = 8
CAPY = 32
Z = 256
X = 256
Y = 512
X2 = 128
Y2 = 256
Z2 = 128
N_GX = 32
N_GY = 16


def live_counts(key, tiles, capacity):
    key_counts, key_full = jax.random.split(key)
    counts = 2 * jax.random.randint(key_counts, (tiles,), capacity // 4, capacity // 2 + 1)
    full_at = jax.random.randint(key_full, (), 0, tiles)
    return jnp.where(jnp.arange(tiles) == full_at, capacity, counts).astype(jnp.int32)


def draw_rows_live(key, part):
    return live_counts(jax.random.fold_in(key, 3), N_GX, CAPX)


def draw_cols_live(key, part):
    return live_counts(jax.random.fold_in(key, 7), N_GY, CAPY)


def raised(drawn, key, source, target, blocks, factor):
    owner, partner = [(jnp.arange(drawn.shape[position]) // (drawn.shape[position] // blocks)).reshape([-1 if axis == position else 1 for axis in range(drawn.ndim)]) for position in (source, target)]
    chosen = jax.random.permutation(key, blocks)[partner]
    strong = (owner == chosen) | (owner == (partner + blocks // 2) % blocks)
    return jnp.where(strong, factor * drawn, drawn)


def steps_of(own_key, extent, cuts, least, high):
    level = 1.0
    for axis_at, shards_of in cuts:
        heights = jax.random.uniform(jax.random.fold_in(jax.random.fold_in(own_key, 6), axis_at), (shards_of,), jnp.float32, least / len(cuts), high / len(cuts))
        level = level * jnp.repeat(jnp.exp(heights), extent[axis_at] // shards_of).reshape((-1,) + (1,) * (len(extent) - 1 - axis_at))
    return level


def normal_values(key, dims, deviation, reach, cuts=(), held_as=jnp.bfloat16):
    result = deviation * jax.random.normal(key, dims, jnp.float32)
    if cuts:
        result = result * steps_of(key, dims, cuts, -0.22, 0.18)
    return jnp.clip(result, -reach, reach).astype(held_as)


def bell_draw_with(key, extent, deviation, most, cuts, heavy, held_as=jnp.bfloat16):
    entries = deviation * jax.random.normal(key, extent, jnp.float32)
    if cuts:
        entries = entries * steps_of(key, extent, cuts, -0.22, 0.18)
    return jnp.clip(raised(entries, jax.random.fold_in(key, 3), *heavy), -most, most).astype(held_as)


def setup_inputs(seed: int = 0) -> dict:
    key_of = jax.random.split(jax.random.key(seed), 7)
    fields = normal_values(key_of[0], (CIN, X, Y, Z), 1.0, 6.0, ((1, 32), (2, 16)))
    rows_live = draw_rows_live(jax.random.fold_in(key_of[6], 71), 0)
    cols_live = draw_cols_live(jax.random.fold_in(key_of[6], 71), 0)
    weight = normal_values(key_of[3], (COUT, CIN * 27), (CIN * 27) ** -0.5, 0.625)
    bias = normal_values(key_of[4], (COUT,), 0.5, 3.0, (), jnp.float32)
    grad_out = bell_draw_with(key_of[5], (COUT, X2, Y2, Z2), (4.0 / (X2 * Y2 * Z2) ** 0.5), 0.0234375, ((0, 16), (1, 32)), (1, 0, 32, 2.75))
    return dict(fields=fields, rows_live=rows_live, cols_live=cols_live, weight=weight, bias=bias, grad_out=grad_out)


def extend(data, border, count, dim):
    length = data.shape[dim]
    border_wide = jnp.expand_dims(border, dim)
    joined = jnp.concatenate([jnp.zeros_like(border_wide), data], axis=dim)
    shape = [1] * joined.ndim
    shape[dim] = length + 1
    places = jnp.arange(length + 1, dtype=jnp.int32).reshape(shape)
    edge_at = length - count
    kept = jnp.where(places > edge_at, joined, jnp.zeros_like(joined))
    return jnp.where(places == edge_at, border_wide, kept)


def taps(padded, axes, halves):
    pieces = []
    for off_x in range(3):
        for off_y in range(3):
            for off_z in range(3):
                piece = padded
                for axis_no, offset, half in zip(axes, (off_x, off_y, off_z), halves):
                    piece = lax.slice_in_dim(piece, offset, offset + 2 * half - 1, 2, axis_no)
                pieces.append(piece)
    return pieces


def reference(fields, rows_live, cols_live, weight, bias, grad_out):
    half_x = CAPX // 2
    half_y = CAPY // 2
    half_z = Z // 2
    grid = fields.reshape(CIN, N_GX, CAPX, N_GY, CAPY, Z)
    last_rows = grid[:, :, CAPX - 1]
    above = jnp.concatenate([jnp.zeros_like(last_rows[:, :1]), last_rows[:, :-1]], axis=1)
    ext_rows = extend(grid, above, rows_live.reshape(1, N_GX, 1, 1, 1, 1), 2)
    last_cols = ext_rows[:, :, :, :, CAPY - 1]
    beside = jnp.concatenate([jnp.zeros_like(last_cols[:, :, :, :1]), last_cols[:, :, :, :-1]], axis=3)
    ext_full = extend(ext_rows, beside, cols_live.reshape(1, 1, 1, N_GY, 1, 1), 4)
    padded = jnp.pad(ext_full, ((0, 0), (0, 0), (0, 0), (0, 0), (0, 0), (1, 0)))
    row_ok = jnp.arange(half_x, dtype=jnp.int32)[None, :] >= half_x - (rows_live // 2)[:, None]
    col_ok = jnp.arange(half_y, dtype=jnp.int32)[None, :] >= half_y - (cols_live // 2)[:, None]
    live = row_ok[:, :, None, None] & col_ok[None, None, :, :]

    def row_taps(index):
        row = lax.dynamic_index_in_dim(padded, index, 1, keepdims=False)
        return jnp.stack(taps(row, (1, 3, 4), (half_x, half_y, half_z)), axis=1).reshape(CIN * 27, -1)

    def forward_row(index):
        conv = jnp.dot(weight, row_taps(index), preferred_element_type=jnp.float32) + bias[:, None]
        keep = lax.dynamic_index_in_dim(live, index, 0, keepdims=False)
        conv = conv.reshape(COUT, half_x, N_GY, half_y, half_z)
        return jnp.where(keep.reshape(1, half_x, N_GY, half_y, 1), conv, 0.0).astype(jnp.bfloat16)

    indices = jnp.arange(N_GX, dtype=jnp.int32)
    pre_rows = lax.map(forward_row, indices)
    pre = jnp.moveaxis(pre_rows, 0, 1).reshape(COUT, X2, Y2, Z2)
    pre_wide = pre.astype(jnp.float32)
    sigma = jax.nn.sigmoid(pre_wide)
    stem = (pre_wide * sigma).astype(jnp.bfloat16)
    slope = sigma * (1.0 + pre_wide * (1.0 - sigma))
    live_all = live.reshape(1, X2, Y2, 1)
    grad_pre = jnp.where(live_all, grad_out.astype(jnp.float32) * slope, 0.0).astype(jnp.bfloat16)
    grad_rows = grad_pre.reshape(COUT, N_GX, half_x, N_GY, half_y, half_z)

    def backward_row(carry, index):
        grad_row = lax.dynamic_index_in_dim(grad_rows, index, 1, keepdims=False).reshape(COUT, -1)
        patches = row_taps(index)
        part = lax.dot_general(grad_row, patches, (((1,), (1,)), ((), ())), preferred_element_type=jnp.float32)
        total = jnp.sum(grad_row.astype(jnp.float32), axis=1)
        return (carry[0] + part, carry[1] + total), None

    start = (jnp.zeros((COUT, CIN * 27), jnp.float32), jnp.zeros((COUT,), jnp.float32))
    (weight_grad, bias_grad), unused = lax.scan(backward_row, start, indices)
    return stem, weight_grad, bias_grad
```

```python
import functools

import jax
import jax.numpy as jnp
from jax import lax
from jax.experimental import pallas as pl
from jax.experimental.pallas import tpu as pltpu
from jax.sharding import PartitionSpec as P

MESH = pl.DeviceIdType.MESH
F32 = jnp.float32
BF16 = jnp.bfloat16
LANES = 128


def nt_dot(a, b):
    return lax.dot_general(a, b, (((1,), (1,)), ((), ())), preferred_element_type=F32)


def kernel(
    dims,
    fields_hbm, rows_ref, cols_ref, weight_ref, bias_ref, grad_hbm,
    stem_hbm, sums_ref,
    fields, above, side, side_in, corner_in, rows32, border, extra, spread, taps_b, diff,
    patches, band, acc, slope, stage, grads, grad_pre, corr, diag,
    part, part_in, xpart, xpart_in, zpart, zpart_in,
    load_sem, halo_send, halo_recv, grad_send, grad_recv, stem_send, stem_recv,
    part_send, part_recv, x_send, x_recv, z_send, z_recv,
):
    nx, ny, span, cin, cout, cap_x, cap_y, depth = dims
    half_x, half_y, half_z = cap_x // 2, cap_y // 2, depth // 2
    own = cout // ny
    planes = nx // span
    cy = cin * cap_y
    body = 9 * cy
    wide = patches.shape[0]
    cells = half_x * half_z

    gx, gy = lax.axis_index("gx"), lax.axis_index("gy")
    iz, ix = gx // span, gx % span

    def wrap(value, size):
        return lax.rem(value + size, size)

    def farthest_first(step):
        half = (step + 1) // 2
        return ny // 2 + jnp.where(step % 2 == 1, half, -half)

    def x_peer(d):
        return (iz * span + wrap(ix + d, span), gy)

    def z_peer(d):
        return (wrap(iz + d, planes) * span + ix, gy)

    barrier = pltpu.get_barrier_semaphore()

    def greet(device):
        pl.semaphore_signal(barrier, inc=1, device_id=device, device_id_type=MESH)

    def greet_y(step, carry):
        greet((gx, wrap(gy + farthest_first(step), ny)))
        return carry

    load = pltpu.make_async_copy(fields_hbm, fields, load_sem.at[0])
    load.start()
    mine = pltpu.make_async_copy(
        grad_hbm.at[:, :, pl.ds(gy * half_y, half_y), :],
        grads.at[pl.ds(gy * own, own)],
        load_sem.at[1],
    )
    mine.start()
    lax.fori_loop(0, ny - 1, greet_y, 0)
    for dx, dy in ((1, 0), (-1, 0), (1, 1), (-1, -1)):
        greet((wrap(gx + dx, nx), wrap(gy + dy, ny)))
    for d in range(1, span):
        greet(x_peer(d))
    for d in range(1, planes):
        greet(z_peer(d))
    pl.semaphore_wait(barrier, ny - 1 + 4 + span - 1 + planes - 1)

    def halo_copy(index, src, dst, dx, dy):
        return pltpu.make_async_remote_copy(
            src_ref=src, dst_ref=dst, send_sem=halo_send.at[index], recv_sem=halo_recv.at[index],
            device_id=(wrap(gx + dx, nx), wrap(gy + dy, ny)), device_id_type=MESH,
        )

    def grad_copy(d):
        to = wrap(gy + d, ny)
        return pltpu.make_async_remote_copy(
            src_ref=grad_hbm.at[:, :, pl.ds(to * half_y, half_y), :],
            dst_ref=grads.at[pl.ds(gy * own, own)],
            send_sem=grad_send.at[d], recv_sem=grad_recv.at[d],
            device_id=(gx, to), device_id_type=MESH,
        )

    load.wait()
    rows_out = halo_copy(0, fields.at[:, cap_x - 1], above, 1, 0)
    rows_out.start()
    for x in range(cap_x):
        for c in range(cin):
            tail = fields[c, x, cap_y - 16:cap_y, :].astype(F32)
            rows32[x * cin + c:x * cin + c + 1, :] = tail[15:16, :]
    side[...] = rows32[...].astype(BF16)
    side_out = halo_copy(1, side, side_in, 0, 1)
    side_out.start()
    corner_out = halo_copy(2, side, corner_in, 1, 1)
    corner_out.start()

    def start_grad(step, carry):
        grad_copy(farthest_first(step)).start()
        return carry

    lax.fori_loop(0, ny - 1, start_grad, 0)

    z_at = lax.broadcasted_iota(jnp.int32, (depth, 3 * half_z), 0)
    n_at = lax.broadcasted_iota(jnp.int32, (depth, 3 * half_z), 1)
    spread[...] = jnp.where(
        z_at == 2 * (n_at % half_z) - 1 + n_at // half_z, 1.0, 0.0
    ).astype(BF16)

    n_row = lax.broadcasted_iota(jnp.int32, (1, wide), 1)
    tail_at = n_row - body
    in_body = tail_at < 0
    in_edge = (tail_at >= 0) & (tail_at < 9 * cin)
    ones_at = tail_at == 9 * cin
    chan = jnp.where(in_body, (n_row // cap_y) % cin, tail_at % cin)
    off = jnp.where(in_body, n_row // cy, tail_at // cin)
    off_x, off_z = off // 3, off % 3
    first_tap = chan * 27 + off_x * 9 + off_z
    ext_y = jnp.where(in_body, n_row % cap_y + 1, jnp.where(in_edge, 0, -1000))
    w_at = lax.broadcasted_iota(jnp.int32, (LANES, wide), 0)
    for b in range(3):
        goal = jnp.where(in_body | in_edge, first_tap + 3 * b, -1)
        if b == 0:
            goal = jnp.where(ones_at, cin * 27, goal)
        taps_b[b] = jnp.where(w_at == goal, 1.0, 0.0).astype(BF16)
    q_at = lax.broadcasted_iota(jnp.int32, (half_y, wide), 0)
    diff[...] = jnp.where(ones_at, 0, ext_y - 2 * q_at)

    for b in range(3):
        corr[b] = jnp.dot(weight_ref[...], taps_b[b, 0:cin * 27, :], preferred_element_type=F32)

    def fill_band(o, carry):
        rows = pl.ds(pl.multiple_of(o * half_y, half_y), half_y)
        value = jnp.zeros((half_y, wide), F32)
        for b in range(3):
            value = jnp.where(diff[...] == b, corr[b, pl.ds(o, 1), :], value)
        band[rows, :] = value.astype(BF16)
        return carry

    lax.fori_loop(0, cout, fill_band, 0)

    rows_out.wait_recv()
    side_out.wait_recv()
    corner_out.wait_recv()
    edge_x = cap_x - rows_ref[gx]
    edge_y = cap_y - cols_ref[gy]
    inner_x = gx > 0
    inner_y = gy > 0
    rows32[...] = side_in[...].astype(F32)
    border[...] = jnp.zeros_like(border)
    corner = corner_in[cin * cap_x - 16:cin * cap_x, :].astype(F32)[16 - cin:16, :]
    for x in range(cap_x + 1):
        line = jnp.where((x == edge_x) & inner_x & inner_y, corner, 0.0)
        if x > 0:
            line = jnp.where((x > edge_x) & inner_y, rows32[(x - 1) * cin:x * cin, :], line)
        border[x * cin:(x + 1) * cin, :] = line
    y_at = lax.broadcasted_iota(jnp.int32, (cap_y, depth), 0) + 1
    for x in range(cap_x + 1):
        blocks = []
        for c in range(cin):
            block = jnp.where((x == edge_x) & inner_x, above[c].astype(F32), 0.0)
            if x > 0:
                block = jnp.where(x > edge_x, fields[c, x - 1].astype(F32), block)
            line = border[x * cin + c:x * cin + c + 1, :]
            block = jnp.where(y_at > edge_y, block, jnp.where(y_at == edge_y, line, 0.0))
            blocks.append(block.astype(BF16))
        split = jnp.dot(
            jnp.concatenate(blocks, axis=0), spread[...], preferred_element_type=F32
        ).astype(BF16)
        for a in range(3):
            if (x - a) % 2 == 0 and 0 <= (x - a) // 2 < half_x:
                p = (x - a) // 2
                for k in range(3):
                    row = (a * 3 + k) * cy
                    patches[row:row + cy, p * half_z:(p + 1) * half_z] = split[:, k * half_z:(k + 1) * half_z]
    before = jnp.where(edge_y == 0, border[...], 0.0).astype(BF16)
    split = jnp.dot(before, spread[...], preferred_element_type=F32)
    extra[...] = jnp.zeros_like(extra)
    for a in range(3):
        for p in range(half_x):
            x = 2 * p + a
            for k in range(3):
                row = (a * 3 + k) * cin
                extra[row:row + cin, p * half_z:(p + 1) * half_z] = (
                    split[x * cin:(x + 1) * cin, k * half_z:(k + 1) * half_z]
                )
    extra[9 * cin:9 * cin + 1, :] = jnp.ones((1, cells), F32)
    patches[body:wide, :] = extra[...].astype(BF16)

    half_rows = cout * half_y // 2

    def multiply(m, carry):
        rows = pl.ds(pl.multiple_of(m * half_rows, half_rows), half_rows)
        acc[rows, :] = jnp.dot(band[rows, :], patches[...], preferred_element_type=F32)
        return carry

    lax.fori_loop(0, 2, multiply, 0)
    q_cell = lax.broadcasted_iota(jnp.int32, (half_y, cells), 0)
    p_cell = lax.broadcasted_iota(jnp.int32, (half_y, cells), 1) // half_z
    live = (2 * q_cell >= edge_y) & (2 * p_cell >= edge_x)

    def stem_copy(d):
        to = wrap(gy + d, ny)
        return pltpu.make_async_remote_copy(
            src_ref=stage.at[pl.ds(to * own, own)],
            dst_ref=stem_hbm.at[:, :, pl.ds(gy * half_y, half_y), :],
            send_sem=stem_send.at[d], recv_sem=stem_recv.at[d],
            device_id=(gx, to), device_id_type=MESH,
        )

    def activate(o):
        rows = pl.ds(pl.multiple_of(o * half_y, half_y), half_y)
        pre = jnp.where(live, acc[rows, :] + bias_ref[o], 0.0).astype(BF16).astype(F32)
        sigma = 1.0 / (1.0 + jnp.exp(-pre))
        value = (pre * sigma).astype(BF16)
        slope[rows, :] = jnp.where(live, sigma * (1.0 + pre * (1.0 - sigma)), 0.0)
        for p in range(half_x):
            stage[o, p] = value[:, p * half_z:(p + 1) * half_z]

    def forward(step, carry):
        d = farthest_first(step)
        for part_of in range(own):
            activate(wrap(gy + d, ny) * own + part_of)
        stem_copy(d).start()
        return carry

    lax.fori_loop(0, ny - 1, forward, 0)
    for part_of in range(own):
        activate(gy * own + part_of)
    keep = pltpu.make_async_copy(
        stage.at[pl.ds(gy * own, own)],
        stem_hbm.at[:, :, pl.ds(gy * half_y, half_y), :],
        load_sem.at[2],
    )
    keep.start()

    mine.wait()

    def wait_grad(d, carry):
        grad_copy(d).wait_recv()
        return carry

    lax.fori_loop(1, ny, wait_grad, 0)

    def chain(o, carry):
        rows = pl.ds(pl.multiple_of(o * half_y, half_y), half_y)
        for p in range(half_x):
            lanes = slice(p * half_z, (p + 1) * half_z)
            grad_pre[rows, lanes] = (grads[o, p].astype(F32) * slope[rows, lanes]).astype(BF16)
        return carry

    lax.fori_loop(0, cout, chain, 0)

    group = diag.shape[0] // half_y

    def correlate(m, carry):
        rows = pl.ds(pl.multiple_of(m * group * half_y, group * half_y), group * half_y)
        diag[...] = nt_dot(grad_pre[rows, :], patches[...])

        def pick(i, inner):
            value = diag[pl.ds(pl.multiple_of(i * half_y, half_y), half_y), :]
            for b in range(3):
                corr[b, pl.ds(m * group + i, 1), :] = jnp.sum(
                    jnp.where(diff[...] == b, value, 0.0), axis=0, keepdims=True
                )
            return inner

        return lax.fori_loop(0, group, pick, carry)

    lax.fori_loop(0, cout // group, correlate, 0)
    total = jnp.zeros((cout, LANES), F32)
    for b in range(3):
        high = corr[b].astype(BF16)
        low = (corr[b] - high.astype(F32)).astype(BF16)
        total = total + (nt_dot(high, taps_b[b]) + nt_dot(low, taps_b[b]))

    part[...] = jnp.zeros_like(part)
    for j in range(ny):
        part[j, 0:own, :] = total[j * own:(j + 1) * own, :]

    def part_copy(d):
        to = wrap(gy + d, ny)
        return pltpu.make_async_remote_copy(
            src_ref=part.at[to], dst_ref=part_in.at[d],
            send_sem=part_send.at[d], recv_sem=part_recv.at[d],
            device_id=(gx, to), device_id_type=MESH,
        )

    def start_part(step, carry):
        part_copy(farthest_first(step)).start()
        return carry

    lax.fori_loop(0, ny - 1, start_part, 0)

    def take_part(d, held):
        part_copy(d).wait_recv()
        return held + part_in[d]

    xpart[...] = lax.fori_loop(1, ny, take_part, part[gy])

    def x_copy(d):
        return pltpu.make_async_remote_copy(
            src_ref=xpart, dst_ref=xpart_in.at[ix],
            send_sem=x_send.at[d], recv_sem=x_recv.at[d],
            device_id=x_peer(d), device_id_type=MESH,
        )

    def z_copy(d):
        return pltpu.make_async_remote_copy(
            src_ref=zpart, dst_ref=zpart_in.at[iz],
            send_sem=z_send.at[d], recv_sem=z_recv.at[d],
            device_id=z_peer(d), device_id_type=MESH,
        )

    for d in range(1, span):
        x_copy(d).start()
    xpart_in[ix] = xpart[...]
    for d in range(1, span):
        x_copy(d).wait_recv()
    zpart[...] = sum([xpart_in[i] for i in range(1, span)], xpart_in[0])
    for d in range(1, planes):
        z_copy(d).start()
    zpart_in[iz] = zpart[...]
    for d in range(1, planes):
        z_copy(d).wait_recv()
    sums_ref[...] = sum([zpart_in[i] for i in range(1, planes)], zpart_in[0])

    def finish(d, carry):
        stem_copy(d).wait_recv()
        stem_copy(d).wait_send()
        grad_copy(d).wait_send()
        part_copy(d).wait_send()
        return carry

    lax.fori_loop(1, ny, finish, 0)
    for d in range(1, span):
        x_copy(d).wait_send()
    for d in range(1, planes):
        z_copy(d).wait_send()
    rows_out.wait_send()
    side_out.wait_send()
    corner_out.wait_send()
    keep.wait()


def local(nx, ny, span, fields, rows_live, cols_live, weight, bias, grad_out):
    cin, cap_x, cap_y, depth = fields.shape
    cout = weight.shape[0]
    half_x, half_y, half_z = cap_x // 2, cap_y // 2, depth // 2
    planes = nx // span
    cells = half_x * half_z
    cy = cin * cap_y
    wide = 9 * cy + LANES
    dims = (nx, ny, span, cin, cout, cap_x, cap_y, depth)
    vmem = pl.BlockSpec(memory_space=pltpu.VMEM)
    smem = pl.BlockSpec(memory_space=pltpu.SMEM)
    hbm = pl.BlockSpec(memory_space=pl.ANY)
    dma = pltpu.SemaphoreType.DMA
    stem, sums = pl.pallas_call(
        functools.partial(kernel, dims),
        out_shape=(
            jax.ShapeDtypeStruct(grad_out.shape, BF16),
            jax.ShapeDtypeStruct((8, LANES), F32),
        ),
        in_specs=[hbm, smem, smem, vmem, smem, hbm],
        out_specs=(hbm, vmem),
        scratch_shapes=[
            pltpu.VMEM((cin, cap_x, cap_y, depth), BF16),
            pltpu.VMEM((cin, cap_y, depth), BF16),
            pltpu.VMEM((cin * cap_x, depth), BF16),
            pltpu.VMEM((cin * cap_x, depth), BF16),
            pltpu.VMEM((cin * cap_x, depth), BF16),
            pltpu.VMEM((cin * cap_x, depth), F32),
            pltpu.VMEM((48, depth), F32),
            pltpu.VMEM((LANES, cells), F32),
            pltpu.VMEM((depth, 3 * half_z), BF16),
            pltpu.VMEM((3, LANES, wide), BF16),
            pltpu.VMEM((half_y, wide), jnp.int32),
            pltpu.VMEM((wide, cells), BF16),
            pltpu.VMEM((cout * half_y, wide), BF16),
            pltpu.VMEM((cout * half_y, cells), F32),
            pltpu.VMEM((cout * half_y, cells), F32),
            pltpu.VMEM((cout, half_x, half_y, half_z), BF16),
            pltpu.VMEM((cout, half_x, half_y, half_z), BF16),
            pltpu.VMEM((cout * half_y, cells), BF16),
            pltpu.VMEM((3, cout, wide), F32),
            pltpu.VMEM((8 * half_y, wide), F32),
            pltpu.VMEM((ny, 8, LANES), F32),
            pltpu.VMEM((ny, 8, LANES), F32),
            pltpu.VMEM((8, LANES), F32),
            pltpu.VMEM((span, 8, LANES), F32),
            pltpu.VMEM((8, LANES), F32),
            pltpu.VMEM((planes, 8, LANES), F32),
            dma((3,)), dma((3,)), dma((3,)),
            dma((ny,)), dma((ny,)), dma((ny,)), dma((ny,)), dma((ny,)), dma((ny,)),
            dma((span,)), dma((span,)), dma((planes,)), dma((planes,)),
        ],
        compiler_params=pltpu.CompilerParams(
            collective_id=0, has_side_effects=True, vmem_limit_bytes=40 * 1024 * 1024
        ),
    )(fields, rows_live, cols_live, weight, bias, grad_out)
    own = cout // ny
    taps = weight.shape[1]
    return stem, sums[:own, :taps], sums[:own, taps]


def solution(mesh):
    nx, ny = mesh.shape["gx"], mesh.shape["gy"]
    span = 4 if nx % 4 == 0 else 1
    in_specs = (P(None, "gx", "gy", None), P(), P(), P(), P(), P("gy", "gx", None, None))
    out_specs = (P("gy", "gx", None, None), P("gy", None), P("gy"))
    run = functools.partial(local, nx, ny, span)
    return jax.shard_map(run, mesh=mesh, in_specs=in_specs, out_specs=out_specs, check_vma=False)
```

```python
import functools

import jax
import jax.numpy as jnp
from jax import lax
from jax.experimental import pallas as pl
from jax.experimental.pallas import tpu as pltpu
from jax.sharding import PartitionSpec as P

MESH = pl.DeviceIdType.MESH
F32 = jnp.float32
BF16 = jnp.bfloat16
LANES = 128
EARLY = 0
SOON = 1
FIRST = 6
GROUP = 4


def nt_dot(a, b):
    return lax.dot_general(a, b, (((1,), (1,)), ((), ())), preferred_element_type=F32)


def kernel(
    dims,
    fields_hbm, rows_hbm, cols_hbm, weight_hbm, bias_hbm, grad_hbm,
    stem_hbm, sums_ref,
    rows_ref, cols_ref, weight_ref, bias_ref, fields, above, side, side_in, corner_in,
    rows32, lines, border, spread, taps_b, band, patches, acc, slope, stage, grads, grad_pre,
    part, part_in, xpart, xpart_in, zpart, zpart_in,
    load_sem, halo_send, halo_recv, grad_send, grad_recv, stem_send, stem_recv,
    part_send, part_recv, x_send, x_recv, z_send, z_recv,
):
    nx, ny, span, cin, cout, cap_x, cap_y, depth = dims
    half_x, half_y, half_z = cap_x // 2, cap_y // 2, depth // 2
    own = cout // ny
    planes = nx // span
    own = cout // ny
    cells = half_x * half_z
    tall = patches.shape[1]
    window = band.shape[1] // 9
    reach = half_y // GROUP

    gx, gy = lax.axis_index("gx"), lax.axis_index("gy")
    iz, ix = gx // span, gx % span

    def wrap(value, size):
        return lax.rem(value + size, size)

    def farthest_first(step):
        half = (step + 1) // 2
        return ny // 2 + jnp.where(step % 2 == 1, half, -half)

    def x_peer(d):
        return (iz * span + wrap(ix + d, span), gy)

    def z_peer(d):
        return (wrap(iz + d, planes) * span + ix, gy)

    barrier = pltpu.get_barrier_semaphore()

    def greet(device):
        pl.semaphore_signal(barrier, inc=1, device_id=device, device_id_type=MESH)

    def greet_y(step, carry):
        greet((gx, wrap(gy + farthest_first(step), ny)))
        return carry

    load = pltpu.make_async_copy(fields_hbm, fields, load_sem.at[0])
    load.start()
    mine = pltpu.make_async_copy(
        grad_hbm.at[:, :, pl.ds(gy * half_y, half_y), :],
        grads.at[pl.ds(gy * own, own)],
        load_sem.at[1],
    )
    mine.start()
    small = [
        pltpu.make_async_copy(src, dst, load_sem.at[3 + i])
        for i, (src, dst) in enumerate(
            ((rows_hbm, rows_ref), (cols_hbm, cols_ref), (weight_hbm, weight_ref), (bias_hbm, bias_ref))
        )
    ]
    for copy in small:
        copy.start()
    lax.fori_loop(0, ny - 1, greet_y, 0)
    for dx, dy in ((1, 0), (-1, 0), (1, 1), (-1, -1)):
        greet((wrap(gx + dx, nx), wrap(gy + dy, ny)))
    for d in range(1, span):
        greet(x_peer(d))
    for d in range(1, planes):
        greet(z_peer(d))
    pl.semaphore_wait(barrier, ny - 1 + 4 + span - 1 + planes - 1)

    def halo_copy(index, src, dst, dx, dy):
        return pltpu.make_async_remote_copy(
            src_ref=src, dst_ref=dst, send_sem=halo_send.at[index], recv_sem=halo_recv.at[index],
            device_id=(wrap(gx + dx, nx), wrap(gy + dy, ny)), device_id_type=MESH,
        )

    def grad_copy(d):
        to = wrap(gy + d, ny)
        return pltpu.make_async_remote_copy(
            src_ref=grad_hbm.at[:, :, pl.ds(to * half_y, half_y), :],
            dst_ref=grads.at[pl.ds(gy * own, own)],
            send_sem=grad_send.at[d], recv_sem=grad_recv.at[d],
            device_id=(gx, to), device_id_type=MESH,
        )

    def start_grad(step, carry):
        grad_copy(farthest_first(step)).start()
        return carry

    rows_out = halo_copy(0, fields_hbm.at[:, cap_x - 1], above, 1, 0)
    rows_out.start()
    lax.fori_loop(0, min(FIRST, ny - 1), start_grad, 0)

    load.wait()
    for x in range(cap_x):
        for c in range(cin):
            for h in range(2):
                lines[x + 1, h, pl.ds(cin + c, cap_y, stride=cin), :] = (
                    fields[c, x, :, h * half_z:(h + 1) * half_z].astype(F32)
                )
        for h in range(2):
            rows32[x * cin:(x + 1) * cin, h * half_z:(h + 1) * half_z] = (
                lines[x + 1, h, cin * cap_y:cin * (cap_y + 1), :]
            )
    side[...] = rows32[...].astype(BF16)
    side_out = halo_copy(1, side, side_in, 0, 1)
    side_out.start()
    corner_out = halo_copy(2, side, corner_in, 1, 1)
    corner_out.start()
    lax.fori_loop(min(FIRST, ny - 1), ny - 1, start_grad, 0)

    z_at = lax.broadcasted_iota(jnp.int32, (depth, 3 * half_z), 0)
    n_at = lax.broadcasted_iota(jnp.int32, (depth, 3 * half_z), 1)
    spread[...] = jnp.where(
        z_at == 2 * (n_at % half_z) - 1 + n_at // half_z, 1.0, 0.0
    ).astype(BF16)

    n_row = lax.broadcasted_iota(jnp.int32, (1, 9 * window), 1)
    off, place = n_row // window, n_row % window
    first_tap = (place % cin) * 27 + (off // 3) * 9 + off % 3
    ext_y = place // cin
    w_at = lax.broadcasted_iota(jnp.int32, (LANES, 9 * window), 0)
    for b in range(3):
        taps_b[b] = jnp.where(w_at == first_tap + 3 * b, 1.0, 0.0).astype(BF16)
    for copy in small:
        copy.wait()

    by_tap = [
        jnp.dot(weight_ref[...], taps_b[b, 0:cin * 27, :], preferred_element_type=F32)
        for b in range(3)
    ]
    for i in range(GROUP):
        value = jnp.zeros((cout, 9 * window), F32)
        for b in range(3):
            value = jnp.where(ext_y == 2 * i + b, by_tap[b], value)
        band[i * cout:(i + 1) * cout, :] = value.astype(BF16)

    rows_out.wait_recv()
    side_out.wait_recv()
    corner_out.wait_recv()
    edge_x = cap_x - rows_ref[gx]
    edge_y = cap_y - cols_ref[gy]
    inner_x = gx > 0
    inner_y = gy > 0
    rows32[...] = side_in[...].astype(F32)
    corner = corner_in[cin * cap_x - 16:cin * cap_x, :].astype(F32)[16 - cin:16, :]
    for x in range(cap_x + 1):
        line = jnp.where((x == edge_x) & inner_x & inner_y, corner, 0.0)
        if x > 0:
            line = jnp.where((x > edge_x) & inner_y, rows32[(x - 1) * cin:x * cin, :], line)
        for i in range(8 // cin):
            border[x, i * cin:(i + 1) * cin, :] = line
    for c in range(cin):
        for h in range(2):
            lines[0, h, pl.ds(cin + c, cap_y, stride=cin), :] = (
                above[c, :, h * half_z:(h + 1) * half_z].astype(F32)
            )
    whole = (tall // 8, 8, half_z)
    y_at = (
        lax.broadcasted_iota(jnp.int32, whole, 0) * 8 + lax.broadcasted_iota(jnp.int32, whole, 1)
    ) // cin
    inside = (y_at > edge_y) & (y_at <= cap_y)
    at_edge = y_at == edge_y
    for x in range(cap_x + 1):
        halves = []
        for h in range(2):
            value = jnp.where((x == edge_x) & inner_x, lines[0, h], 0.0)
            if x > 0:
                value = jnp.where(x > edge_x, lines[x, h], value)
            line = border[x, :, h * half_z:(h + 1) * half_z][None]
            value = jnp.where(inside, value.reshape(whole), jnp.where(at_edge, line, 0.0))
            halves.append(value.reshape(tall, half_z).astype(BF16))
        value = jnp.concatenate(halves, axis=1)
        split = jnp.dot(
            value, spread[...], preferred_element_type=F32
        ).astype(BF16)
        for a in range(3):
            if (x - a) % 2 == 0 and 0 <= (x - a) // 2 < half_x:
                p = (x - a) // 2
                for k in range(3):
                    patches[a * 3 + k, :, p * half_z:(p + 1) * half_z] = (
                        split[:, k * half_z:(k + 1) * half_z]
                    )

    def windows(m):
        first = 2 * GROUP * cin * m
        return patches[:, first:first + window, :].reshape(9 * window, cells)

    for m in range(reach):
        value = jnp.dot(band[...], windows(m), preferred_element_type=F32)
        for i in range(GROUP):
            for p in range(half_x):
                acc[p, pl.ds(m * GROUP + i, cout, stride=half_y), :] = (
                    value[i * cout:(i + 1) * cout, p * half_z:(p + 1) * half_z]
                )
    q_live = 2 * lax.broadcasted_iota(jnp.int32, (half_y, half_z), 0) >= edge_y

    def stem_copy(d):
        to = wrap(gy + d, ny)
        return pltpu.make_async_remote_copy(
            src_ref=stage.at[pl.ds(to * own, own)],
            dst_ref=stem_hbm.at[:, :, pl.ds(gy * half_y, half_y), :],
            send_sem=stem_send.at[d], recv_sem=stem_recv.at[d],
            device_id=(gx, to), device_id_type=MESH,
        )

    def activate(o):
        rows = pl.ds(pl.multiple_of(o * half_y, half_y), half_y)
        for p in range(half_x):
            live = q_live & (2 * p >= edge_x)
            pre = jnp.where(live, acc[p, rows, :] + bias_ref[o], 0.0).astype(BF16).astype(F32)
            sigma = 1.0 / (1.0 + jnp.exp(-pre))
            stage[o, p] = (pre * sigma).astype(BF16)
            slope[p, rows, :] = jnp.where(live, sigma * (1.0 + pre * (1.0 - sigma)), 0.0)

    def forward(step, carry):
        d = farthest_first(step)
        for part_of in range(own):
            activate(wrap(gy + d, ny) * own + part_of)
        return carry

    def start_stem(step, carry):
        stem_copy(farthest_first(step)).start()
        return carry

    lax.fori_loop(0, ny - 1, forward, 0)
    for part_of in range(own):
        activate(gy * own + part_of)
    lax.fori_loop(0, min(EARLY, ny - 1), start_stem, 0)
    keep = pltpu.make_async_copy(
        stage.at[pl.ds(gy * own, own)],
        stem_hbm.at[:, :, pl.ds(gy * half_y, half_y), :],
        load_sem.at[2],
    )
    keep.start()

    mine.wait()

    def wait_grad(d, carry):
        grad_copy(d).wait_recv()
        return carry

    lax.fori_loop(1, ny, wait_grad, 0)
    lax.fori_loop(min(EARLY, ny - 1), min(SOON, ny - 1), start_stem, 0)

    def chain(o, carry):
        rows = pl.ds(pl.multiple_of(o * half_y, half_y), half_y)
        for p in range(half_x):
            value = (grads[o, p].astype(F32) * slope[p, rows, :]).astype(BF16)
            grad_pre[p, rows, :] = value.astype(F32)
        return carry

    lax.fori_loop(0, cout, chain, 0)

    corr = jnp.zeros((GROUP * cout, 9 * window), F32)
    bias_sum = jnp.zeros((cout, cells), F32)
    for m in range(reach):
        values = [
            jnp.concatenate(
                [
                    grad_pre[p, pl.ds(m * GROUP + i, cout, stride=half_y), :]
                    for p in range(half_x)
                ],
                axis=1,
            )
            for i in range(GROUP)
        ]
        bias_sum = bias_sum + sum(values[1:], values[0])
        corr = corr + nt_dot(jnp.concatenate(values, axis=0).astype(BF16), windows(m))
    total = jnp.zeros((cout, LANES), F32)
    for b in range(3):
        picked = jnp.zeros((cout, 9 * window), F32)
        for i in range(GROUP):
            picked = jnp.where(ext_y == 2 * i + b, corr[i * cout:(i + 1) * cout, :], picked)
        high = picked.astype(BF16)
        low = (picked - high.astype(F32)).astype(BF16)
        total = total + (nt_dot(high, taps_b[b]) + nt_dot(low, taps_b[b]))
    lane = lax.broadcasted_iota(jnp.int32, (cout, LANES), 1)
    total = jnp.where(lane == cin * 27, jnp.sum(bias_sum, axis=1, keepdims=True), total)

    for j in range(ny):
        part[j] = total[j * own:(j + 1) * own, :]

    def part_copy(d):
        to = wrap(gy + d, ny)
        return pltpu.make_async_remote_copy(
            src_ref=part.at[to], dst_ref=part_in.at[d],
            send_sem=part_send.at[d], recv_sem=part_recv.at[d],
            device_id=(gx, to), device_id_type=MESH,
        )

    def start_part(step, carry):
        part_copy(farthest_first(step)).start()
        return carry

    lax.fori_loop(0, ny - 1, start_part, 0)
    lax.fori_loop(min(SOON, ny - 1), ny - 1, start_stem, 0)

    def take_part(d, held):
        part_copy(d).wait_recv()
        return held + part_in[d]

    xpart[...] = lax.fori_loop(1, ny, take_part, part[gy])

    def x_copy(d):
        return pltpu.make_async_remote_copy(
            src_ref=xpart, dst_ref=xpart_in.at[ix],
            send_sem=x_send.at[d], recv_sem=x_recv.at[d],
            device_id=x_peer(d), device_id_type=MESH,
        )

    def z_copy(d):
        return pltpu.make_async_remote_copy(
            src_ref=zpart, dst_ref=zpart_in.at[iz],
            send_sem=z_send.at[d], recv_sem=z_recv.at[d],
            device_id=z_peer(d), device_id_type=MESH,
        )

    for d in range(1, span):
        x_copy(d).start()
    xpart_in[ix] = xpart[...]
    for d in range(1, span):
        x_copy(d).wait_recv()
    zpart[...] = sum([xpart_in[i] for i in range(1, span)], xpart_in[0])
    for d in range(1, planes):
        z_copy(d).start()
    zpart_in[iz] = zpart[...]
    for d in range(1, planes):
        z_copy(d).wait_recv()
    sums_ref[...] = sum([zpart_in[i] for i in range(1, planes)], zpart_in[0])

    def finish(d, carry):
        stem_copy(d).wait_recv()
        stem_copy(d).wait_send()
        grad_copy(d).wait_send()
        part_copy(d).wait_send()
        return carry

    lax.fori_loop(1, ny, finish, 0)
    for d in range(1, span):
        x_copy(d).wait_send()
    for d in range(1, planes):
        z_copy(d).wait_send()
    rows_out.wait_send()
    side_out.wait_send()
    corner_out.wait_send()
    keep.wait()


def hand_over(own, taps, landed, sums, stem, weight_grad, bias_grad, scalars, sem):
    out = pltpu.make_async_copy(landed, stem, sem.at[0])
    out.start()
    read = pltpu.make_async_copy(sums, scalars, sem.at[1])
    read.start()
    weight_grad[...] = sums[0:own, 0:taps]
    read.wait()
    for i in range(own):
        bias_grad[i] = scalars[i, taps]
    out.wait()


def local(nx, ny, span, fields, rows_live, cols_live, weight, bias, grad_out):
    cin, cap_x, cap_y, depth = fields.shape
    cout = weight.shape[0]
    half_x, half_y, half_z = cap_x // 2, cap_y // 2, depth // 2
    planes = nx // span
    own = cout // ny
    cells = half_x * half_z
    tall = cin * (cap_y + 4)
    window = -(-(2 * GROUP + 1) * cin // 16) * 16
    dims = (nx, ny, span, cin, cout, cap_x, cap_y, depth)
    vmem = pl.BlockSpec(memory_space=pltpu.VMEM)
    hbm = pl.BlockSpec(memory_space=pl.ANY)
    dma = pltpu.SemaphoreType.DMA
    landed, sums = pl.pallas_call(
        functools.partial(kernel, dims),
        out_shape=(
            pltpu.VMEM(grad_out.shape, BF16),
            pltpu.VMEM((own, LANES), F32),
        ),
        in_specs=[hbm] * 6,
        out_specs=(vmem, vmem),
        scratch_shapes=[
            pltpu.SMEM(rows_live.shape, jnp.int32),
            pltpu.SMEM(cols_live.shape, jnp.int32),
            pltpu.VMEM(weight.shape, BF16),
            pltpu.SMEM(bias.shape, F32),
            pltpu.VMEM((cin, cap_x, cap_y, depth), BF16),
            pltpu.VMEM((cin, cap_y, depth), BF16),
            pltpu.VMEM((cin * cap_x, depth), BF16),
            pltpu.VMEM((cin * cap_x, depth), BF16),
            pltpu.VMEM((cin * cap_x, depth), BF16),
            pltpu.VMEM((cin * cap_x, depth), F32),
            pltpu.VMEM((cap_x + 1, 2, tall, half_z), F32),
            pltpu.VMEM((cap_x + 1, 8, depth), F32),
            pltpu.VMEM((depth, 3 * half_z), BF16),
            pltpu.VMEM((3, LANES, 9 * window), BF16),
            pltpu.VMEM((GROUP * cout, 9 * window), BF16),
            pltpu.VMEM((9, tall, cells), BF16),
            pltpu.VMEM((half_x, cout * half_y, half_z), F32),
            pltpu.VMEM((half_x, cout * half_y, half_z), F32),
            pltpu.VMEM((cout, half_x, half_y, half_z), BF16),
            pltpu.VMEM((cout, half_x, half_y, half_z), BF16),
            pltpu.VMEM((half_x, cout * half_y, half_z), F32),
            pltpu.VMEM((ny, own, LANES), F32),
            pltpu.VMEM((ny, own, LANES), F32),
            pltpu.VMEM((own, LANES), F32),
            pltpu.VMEM((span, own, LANES), F32),
            pltpu.VMEM((own, LANES), F32),
            pltpu.VMEM((planes, own, LANES), F32),
            dma((7,)), dma((3,)), dma((3,)),
            dma((ny,)), dma((ny,)), dma((ny,)), dma((ny,)), dma((ny,)), dma((ny,)),
            dma((span,)), dma((span,)), dma((planes,)), dma((planes,)),
        ],
        compiler_params=pltpu.CompilerParams(
            collective_id=0, has_side_effects=True, vmem_limit_bytes=63 * 1024 * 1024
        ),
    )(fields, rows_live, cols_live, weight, bias, grad_out)
    taps = weight.shape[1]
    return pl.pallas_call(
        functools.partial(hand_over, own, taps),
        out_shape=(
            jax.ShapeDtypeStruct(grad_out.shape, BF16),
            jax.ShapeDtypeStruct((own, taps), F32),
            jax.ShapeDtypeStruct((own,), F32),
        ),
        in_specs=[vmem, vmem],
        out_specs=(hbm, vmem, pl.BlockSpec(memory_space=pltpu.SMEM)),
        scratch_shapes=[pltpu.SMEM((own, LANES), F32), dma((2,))],
        compiler_params=pltpu.CompilerParams(vmem_limit_bytes=4 * 1024 * 1024),
    )(landed, sums)


def solution(mesh):
    nx, ny = mesh.shape["gx"], mesh.shape["gy"]
    span = 4 if nx % 4 == 0 else 1
    in_specs = (P(None, "gx", "gy", None), P(), P(), P(), P(), P("gy", "gx", None, None))
    out_specs = (P("gy", "gx", None, None), P("gy", None), P("gy"))
    run = functools.partial(local, nx, ny, span)
    return jax.shard_map(run, mesh=mesh, in_specs=in_specs, out_specs=out_specs, check_vma=False)
```

```python
import functools

import jax
import jax.numpy as jnp
from jax import lax
from jax.experimental import pallas as pl
from jax.experimental.pallas import tpu as pltpu
from jax.sharding import PartitionSpec as P

MESH = pl.DeviceIdType.MESH
F32 = jnp.float32
BF16 = jnp.bfloat16
LANES = 128
AFTER = 8
CUTS = (2, 6, 10)
FIRST = 6
GROUP = 4


def nt_dot(a, b):
    return lax.dot_general(a, b, (((1,), (1,)), ((), ())), preferred_element_type=F32)


def kernel(
    dims,
    fields_hbm, rows_hbm, cols_hbm, weight_hbm, bias_hbm, grad_hbm,
    stem_hbm, sums_ref,
    rows_ref, cols_ref, weight_ref, bias_ref, fields, above, side, side_in, corner_in,
    rows32, lines, border, spread, taps_b, band, patches, acc, slope, stage, grads, grad_pre,
    part, part_in, xpart, xpart_in, zpart, zpart_in,
    load_sem, halo_send, halo_recv, grad_send, grad_recv, stem_send, stem_recv,
    part_send, part_recv, x_send, x_recv, z_send, z_recv, seam_sem, told_sem,
):
    nx, ny, span, cin, cout, cap_x, cap_y, depth = dims
    half_x, half_y, half_z = cap_x // 2, cap_y // 2, depth // 2
    own = cout // ny
    planes = nx // span
    own = cout // ny
    half = planes // 2
    cells = half_x * half_z
    tall = patches.shape[1]
    window = band.shape[1] // 9
    reach = half_y // GROUP

    gx, gy = lax.axis_index("gx"), lax.axis_index("gy")
    iz, ix = gx // span, gx % span

    at_seam = (iz == half - 1) | (iz == half)
    across = jnp.where(iz == half, gx - span, gx + span)

    def wrap(value, size):
        return jnp.where(value >= size, value - size, value)

    order = [ny // 2]
    for step in range(1, ny // 2):
        order += [ny // 2 + step, ny // 2 - step]

    def x_peer(d):
        return (iz * span + wrap(ix + d, span), gy)

    def half_peer(d):
        return ((iz // half * half + wrap(iz % half + d, half)) * span + ix, gy)

    def z_peer(d):
        return (wrap(iz + d, planes) * span + ix, gy)

    barrier = pltpu.get_barrier_semaphore()

    def greet(device):
        pl.semaphore_signal(barrier, inc=1, device_id=device, device_id_type=MESH)

    for d in order:
        greet((gx, wrap(gy + d, ny)))
    above_us, below_us = gx > 0, gx < nx - 1

    @pl.when(above_us)
    def _():
        greet((gx - 1, gy))
        greet((gx - 1, wrap(gy + ny - 1, ny)))

    @pl.when(below_us)
    def _():
        greet((gx + 1, gy))
        greet((gx + 1, wrap(gy + 1, ny)))

    for d in range(1, span):
        greet(x_peer(d))
    for d in range(1, half):
        greet(half_peer(d))
    if half:
        @pl.when(at_seam)
        def _():
            greet((across, gy))

    load = pltpu.make_async_copy(fields_hbm, fields, load_sem.at[0])
    load.start()
    mine = pltpu.make_async_copy(
        grad_hbm.at[:, :, pl.ds(gy * half_y, half_y), :],
        grads.at[pl.ds(gy * own, own)],
        load_sem.at[1],
    )
    mine.start()
    small = [
        pltpu.make_async_copy(src, dst, load_sem.at[3 + i])
        for i, (src, dst) in enumerate(
            ((rows_hbm, rows_ref), (cols_hbm, cols_ref), (weight_hbm, weight_ref), (bias_hbm, bias_ref))
        )
    ]
    for copy in small:
        copy.start()
    guests = ny - 1 + span - 1
    guests = guests + jnp.where(above_us, 2, 0) + jnp.where(below_us, 2, 0)
    if half:
        guests = guests + half - 1 + jnp.where(at_seam, 1, 0)
    pl.semaphore_wait(barrier, guests)

    def halo_copy(index, src, dst, dx, dy):
        return pltpu.make_async_remote_copy(
            src_ref=src, dst_ref=dst, send_sem=halo_send.at[index], recv_sem=halo_recv.at[index],
            device_id=(gx + dx, wrap(gy + dy, ny)), device_id_type=MESH,
        )

    def grad_copy(d):
        to = wrap(gy + d, ny)
        return pltpu.make_async_remote_copy(
            src_ref=grad_hbm.at[:, :, pl.ds(to * half_y, half_y), :],
            dst_ref=grads.at[pl.ds(gy * own, own)],
            send_sem=grad_send.at[d], recv_sem=grad_recv.at[d],
            device_id=(gx, to), device_id_type=MESH,
        )

    rows_out = halo_copy(0, fields_hbm.at[:, cap_x - 1], above, 1, 0)

    @pl.when(below_us)
    def _():
        rows_out.start()

    for d in order[:FIRST]:
        grad_copy(d).start()

    load.wait()
    for x in range(cap_x):
        for c in range(cin):
            for h in range(2):
                lines[x + 1, h, pl.ds(cin + c, cap_y, stride=cin), :] = (
                    fields[c, x, :, h * half_z:(h + 1) * half_z].astype(F32)
                )
        for h in range(2):
            rows32[x * cin:(x + 1) * cin, h * half_z:(h + 1) * half_z] = (
                lines[x + 1, h, cin * cap_y:cin * (cap_y + 1), :]
            )
    side[...] = rows32[...].astype(BF16)
    side_out = halo_copy(1, side, side_in, 0, 1)
    side_out.start()
    corner_out = halo_copy(2, side, corner_in, 1, 1)

    @pl.when(below_us)
    def _():
        corner_out.start()

    for d in order[FIRST:]:
        grad_copy(d).start()

    if half:
        @pl.when(at_seam)
        def _():
            pl.semaphore_signal(seam_sem, inc=1, device_id=(across, gy), device_id_type=MESH)

    z_at = lax.broadcasted_iota(jnp.int32, (depth, 3 * half_z), 0)
    n_at = lax.broadcasted_iota(jnp.int32, (depth, 3 * half_z), 1)
    spread[...] = jnp.where(
        z_at == 2 * (n_at % half_z) - 1 + n_at // half_z, 1.0, 0.0
    ).astype(BF16)

    n_row = lax.broadcasted_iota(jnp.int32, (1, 9 * window), 1)
    off, place = n_row // window, n_row % window
    first_tap = (place % cin) * 27 + (off // 3) * 9 + off % 3
    ext_y = place // cin
    w_at = lax.broadcasted_iota(jnp.int32, (LANES, 9 * window), 0)
    for b in range(3):
        taps_b[b] = jnp.where(w_at == first_tap + 3 * b, 1.0, 0.0).astype(BF16)
    for copy in small:
        copy.wait()

    by_tap = [
        jnp.dot(weight_ref[...], taps_b[b, 0:cin * 27, :], preferred_element_type=F32)
        for b in range(3)
    ]
    for i in range(GROUP):
        value = jnp.zeros((cout, 9 * window), F32)
        for b in range(3):
            value = jnp.where(ext_y == 2 * i + b, by_tap[b], value)
        band[i * cout:(i + 1) * cout, :] = value.astype(BF16)

    side_out.wait_recv()

    @pl.when(above_us)
    def _():
        rows_out.wait_recv()
        corner_out.wait_recv()

    edge_x = cap_x - rows_ref[gx]
    edge_y = cap_y - cols_ref[gy]
    inner_x = gx > 0
    inner_y = gy > 0
    rows32[...] = side_in[...].astype(F32)
    corner = corner_in[cin * cap_x - 16:cin * cap_x, :].astype(F32)[16 - cin:16, :]
    for x in range(cap_x + 1):
        line = jnp.where((x == edge_x) & inner_x & inner_y, corner, 0.0)
        if x > 0:
            line = jnp.where((x > edge_x) & inner_y, rows32[(x - 1) * cin:x * cin, :], line)
        for i in range(8 // cin):
            border[x, i * cin:(i + 1) * cin, :] = line
    for c in range(cin):
        for h in range(2):
            lines[0, h, pl.ds(cin + c, cap_y, stride=cin), :] = (
                above[c, :, h * half_z:(h + 1) * half_z].astype(F32)
            )
    whole = (tall // 8, 8, half_z)
    y_at = (
        lax.broadcasted_iota(jnp.int32, whole, 0) * 8 + lax.broadcasted_iota(jnp.int32, whole, 1)
    ) // cin
    inside = (y_at > edge_y) & (y_at <= cap_y)
    at_edge = y_at == edge_y
    for x in range(cap_x + 1):
        halves = []
        for h in range(2):
            value = jnp.where((x == edge_x) & inner_x, lines[0, h], 0.0)
            if x > 0:
                value = jnp.where(x > edge_x, lines[x, h], value)
            line = border[x, :, h * half_z:(h + 1) * half_z][None]
            value = jnp.where(inside, value.reshape(whole), jnp.where(at_edge, line, 0.0))
            halves.append(value.reshape(tall, half_z).astype(BF16))
        value = jnp.concatenate(halves, axis=1)
        split = jnp.dot(
            value, spread[...], preferred_element_type=F32
        ).astype(BF16)
        for a in range(3):
            if (x - a) % 2 == 0 and 0 <= (x - a) // 2 < half_x:
                p = (x - a) // 2
                for k in range(3):
                    patches[a * 3 + k, :, p * half_z:(p + 1) * half_z] = (
                        split[:, k * half_z:(k + 1) * half_z]
                    )

    def windows(m):
        first = 2 * GROUP * cin * m
        return patches[:, first:first + window, :].reshape(9 * window, cells)

    for m in range(reach):
        value = jnp.dot(band[...], windows(m), preferred_element_type=F32)
        for i in range(GROUP):
            for p in range(half_x):
                acc[p, pl.ds(m * GROUP + i, cout, stride=half_y), :] = (
                    value[i * cout:(i + 1) * cout, p * half_z:(p + 1) * half_z]
                )
    q_live = 2 * lax.broadcasted_iota(jnp.int32, (half_y, half_z), 0) >= edge_y

    def stem_copy(d):
        to = wrap(gy + d, ny)
        return pltpu.make_async_remote_copy(
            src_ref=stage.at[pl.ds(to * own, own)],
            dst_ref=stem_hbm.at[:, :, pl.ds(gy * half_y, half_y), :],
            send_sem=stem_send.at[d], recv_sem=stem_recv.at[d],
            device_id=(gx, to), device_id_type=MESH,
        )

    def activate(o):
        rows = pl.ds(pl.multiple_of(o * half_y, half_y), half_y)
        for p in range(half_x):
            live = q_live & (2 * p >= edge_x)
            pre = jnp.where(live, acc[p, rows, :] + bias_ref[o], 0.0).astype(BF16).astype(F32)
            sigma = 1.0 / (1.0 + jnp.exp(-pre))
            stage[o, p] = (pre * sigma).astype(BF16)
            slope[p, rows, :] = jnp.where(live, sigma * (1.0 + pre * (1.0 - sigma)), 0.0)

    def forward(o, carry):
        activate(o)
        return carry

    lax.fori_loop(0, cout, forward, 0)
    keep = pltpu.make_async_copy(
        stage.at[pl.ds(gy * own, own)],
        stem_hbm.at[:, :, pl.ds(gy * half_y, half_y), :],
        load_sem.at[2],
    )
    keep.start()

    if half:
        @pl.when(at_seam)
        def _():
            pl.semaphore_wait(seam_sem, 1)
            for d in range(1, half):
                pl.semaphore_signal(
                    told_sem, inc=1, device_id=half_peer(d), device_id_type=MESH
                )

    mine.wait()

    for d in order[:AFTER]:
        grad_copy(d).wait_recv()
    for d in order[:CUTS[0]]:
        stem_copy(d).start()
    for d in order[AFTER:]:
        grad_copy(d).wait_recv()

    def chain(o, carry):
        rows = pl.ds(pl.multiple_of(o * half_y, half_y), half_y)
        for p in range(half_x):
            value = (grads[o, p].astype(F32) * slope[p, rows, :]).astype(BF16)
            grad_pre[p, rows, :] = value.astype(F32)
        return carry

    lax.fori_loop(0, cout, chain, 0)

    corr = jnp.zeros((GROUP * cout, 9 * window), F32)
    bias_sum = jnp.zeros((cout, cells), F32)
    for m in range(reach):
        values = [
            jnp.concatenate(
                [
                    grad_pre[p, pl.ds(m * GROUP + i, cout, stride=half_y), :]
                    for p in range(half_x)
                ],
                axis=1,
            )
            for i in range(GROUP)
        ]
        bias_sum = bias_sum + sum(values[1:], values[0])
        corr = corr + nt_dot(jnp.concatenate(values, axis=0).astype(BF16), windows(m))
    total = jnp.zeros((cout, LANES), F32)
    for b in range(3):
        picked = jnp.zeros((cout, 9 * window), F32)
        for i in range(GROUP):
            picked = jnp.where(ext_y == 2 * i + b, corr[i * cout:(i + 1) * cout, :], picked)
        high = picked.astype(BF16)
        low = (picked - high.astype(F32)).astype(BF16)
        total = total + (nt_dot(high, taps_b[b]) + nt_dot(low, taps_b[b]))
    lane = lax.broadcasted_iota(jnp.int32, (cout, LANES), 1)
    total = jnp.where(lane == cin * 27, jnp.sum(bias_sum, axis=1, keepdims=True), total)

    for j in range(ny):
        part[j] = total[j * own:(j + 1) * own, :]

    def part_copy(d):
        to = wrap(gy + d, ny)
        return pltpu.make_async_remote_copy(
            src_ref=part.at[to], dst_ref=part_in.at[d],
            send_sem=part_send.at[d], recv_sem=part_recv.at[d],
            device_id=(gx, to), device_id_type=MESH,
        )

    for d in order:
        part_copy(d).start()
    for d in order[CUTS[0]:CUTS[1]]:
        stem_copy(d).start()
    held = part[gy]
    for d in order:
        part_copy(d).wait_recv()
        held = held + part_in[d]
    xpart[...] = held

    def x_copy(d):
        return pltpu.make_async_remote_copy(
            src_ref=xpart, dst_ref=xpart_in.at[ix],
            send_sem=x_send.at[d], recv_sem=x_recv.at[d],
            device_id=x_peer(d), device_id_type=MESH,
        )

    def z_copy(d):
        return pltpu.make_async_remote_copy(
            src_ref=zpart, dst_ref=zpart_in.at[iz],
            send_sem=z_send.at[d], recv_sem=z_recv.at[d],
            device_id=z_peer(d), device_id_type=MESH,
        )

    for d in range(1, span):
        x_copy(d).start()
    for d in order[CUTS[1]:CUTS[2]]:
        stem_copy(d).start()
    xpart_in[ix] = xpart[...]
    for d in range(1, span):
        x_copy(d).wait_recv()
    zpart[...] = sum([xpart_in[i] for i in range(1, span)], xpart_in[0])
    if half:
        @pl.when(jnp.logical_not(at_seam))
        def _():
            pl.semaphore_wait(told_sem, 1)

    for d in range(1, planes):
        z_copy(d).start()
    for d in order[CUTS[2]:]:
        stem_copy(d).start()
    zpart_in[iz] = zpart[...]
    for d in range(1, planes):
        z_copy(d).wait_recv()
    sums_ref[...] = sum([zpart_in[i] for i in range(1, planes)], zpart_in[0])

    for d in order:
        stem_copy(d).wait_recv()
        stem_copy(d).wait_send()
        grad_copy(d).wait_send()
        part_copy(d).wait_send()
    for d in range(1, span):
        x_copy(d).wait_send()
    for d in range(1, planes):
        z_copy(d).wait_send()
    side_out.wait_send()

    @pl.when(below_us)
    def _():
        rows_out.wait_send()
        corner_out.wait_send()

    keep.wait()


def hand_over(own, taps, landed, sums, stem, weight_grad, bias_grad, scalars, sem):
    out = pltpu.make_async_copy(landed, stem, sem.at[0])
    out.start()
    read = pltpu.make_async_copy(sums, scalars, sem.at[1])
    read.start()
    weight_grad[...] = sums[0:own, 0:taps]
    read.wait()
    for i in range(own):
        bias_grad[i] = scalars[i, taps]
    out.wait()


def local(nx, ny, span, fields, rows_live, cols_live, weight, bias, grad_out):
    cin, cap_x, cap_y, depth = fields.shape
    cout = weight.shape[0]
    half_x, half_y, half_z = cap_x // 2, cap_y // 2, depth // 2
    planes = nx // span
    own = cout // ny
    cells = half_x * half_z
    tall = cin * (cap_y + 4)
    window = -(-(2 * GROUP + 1) * cin // 16) * 16
    dims = (nx, ny, span, cin, cout, cap_x, cap_y, depth)
    vmem = pl.BlockSpec(memory_space=pltpu.VMEM)
    hbm = pl.BlockSpec(memory_space=pl.ANY)
    dma = pltpu.SemaphoreType.DMA
    landed, sums = pl.pallas_call(
        functools.partial(kernel, dims),
        out_shape=(
            pltpu.VMEM(grad_out.shape, BF16),
            pltpu.VMEM((own, LANES), F32),
        ),
        in_specs=[hbm] * 6,
        out_specs=(vmem, vmem),
        scratch_shapes=[
            pltpu.SMEM(rows_live.shape, jnp.int32),
            pltpu.SMEM(cols_live.shape, jnp.int32),
            pltpu.VMEM(weight.shape, BF16),
            pltpu.SMEM(bias.shape, F32),
            pltpu.VMEM((cin, cap_x, cap_y, depth), BF16),
            pltpu.VMEM((cin, cap_y, depth), BF16),
            pltpu.VMEM((cin * cap_x, depth), BF16),
            pltpu.VMEM((cin * cap_x, depth), BF16),
            pltpu.VMEM((cin * cap_x, depth), BF16),
            pltpu.VMEM((cin * cap_x, depth), F32),
            pltpu.VMEM((cap_x + 1, 2, tall, half_z), F32),
            pltpu.VMEM((cap_x + 1, 8, depth), F32),
            pltpu.VMEM((depth, 3 * half_z), BF16),
            pltpu.VMEM((3, LANES, 9 * window), BF16),
            pltpu.VMEM((GROUP * cout, 9 * window), BF16),
            pltpu.VMEM((9, tall, cells), BF16),
            pltpu.VMEM((half_x, cout * half_y, half_z), F32),
            pltpu.VMEM((half_x, cout * half_y, half_z), F32),
            pltpu.VMEM((cout, half_x, half_y, half_z), BF16),
            pltpu.VMEM((cout, half_x, half_y, half_z), BF16),
            pltpu.VMEM((half_x, cout * half_y, half_z), F32),
            pltpu.VMEM((ny, own, LANES), F32),
            pltpu.VMEM((ny, own, LANES), F32),
            pltpu.VMEM((own, LANES), F32),
            pltpu.VMEM((span, own, LANES), F32),
            pltpu.VMEM((own, LANES), F32),
            pltpu.VMEM((planes, own, LANES), F32),
            dma((7,)), dma((3,)), dma((3,)),
            dma((ny,)), dma((ny,)), dma((ny,)), dma((ny,)), dma((ny,)), dma((ny,)),
            dma((span,)), dma((span,)), dma((planes,)), dma((planes,)),
            pltpu.SemaphoreType.REGULAR, pltpu.SemaphoreType.REGULAR,
        ],
        compiler_params=pltpu.CompilerParams(
            collective_id=0, has_side_effects=True, vmem_limit_bytes=63 * 1024 * 1024
        ),
    )(fields, rows_live, cols_live, weight, bias, grad_out)
    taps = weight.shape[1]
    return pl.pallas_call(
        functools.partial(hand_over, own, taps),
        out_shape=(
            jax.ShapeDtypeStruct(grad_out.shape, BF16),
            jax.ShapeDtypeStruct((own, taps), F32),
            jax.ShapeDtypeStruct((own,), F32),
        ),
        in_specs=[vmem, vmem],
        out_specs=(hbm, vmem, pl.BlockSpec(memory_space=pltpu.SMEM)),
        scratch_shapes=[pltpu.SMEM((own, LANES), F32), dma((2,))],
        compiler_params=pltpu.CompilerParams(vmem_limit_bytes=4 * 1024 * 1024),
    )(landed, sums)


def solution(mesh):
    nx, ny = mesh.shape["gx"], mesh.shape["gy"]
    span = 4 if nx % 4 == 0 else 1
    in_specs = (P(None, "gx", "gy", None), P(), P(), P(), P(), P("gy", "gx", None, None))
    out_specs = (P("gy", "gx", None, None), P("gy", None), P("gy"))
    run = functools.partial(local, nx, ny, span)
    return jax.shard_map(run, mesh=mesh, in_specs=in_specs, out_specs=out_specs, check_vma=False)
```

```python
import functools

import jax
import jax.numpy as jnp
from jax import lax
from jax.experimental import pallas as pl
from jax.experimental.pallas import tpu as pltpu
from jax.sharding import PartitionSpec as P

MESH = pl.DeviceIdType.MESH
F32 = jnp.float32
BF16 = jnp.bfloat16
LANES = 128
CUTS = (1, 3, 7)
FIRST = 6
GROUP = 4


def nt_dot(a, b):
    return lax.dot_general(a, b, (((1,), (1,)), ((), ())), preferred_element_type=F32)


def kernel(
    dims,
    fields_hbm, rows_hbm, cols_hbm, weight_hbm, bias_hbm, grad_hbm,
    stem_hbm, sums_ref,
    rows_ref, cols_ref, weight_ref, bias_ref, fields, above, side, side_in, corner_in,
    rows32, lines, border, spread, taps_b, band, patches, acc, slope, stage, grads, grad_pre,
    part, part_in, xpart, xpart_in, zpart, zpart_in,
    load_sem, halo_send, halo_recv, grad_send, grad_recv, stem_send, stem_recv,
    part_send, part_recv, x_send, x_recv, z_send, z_recv, seam_sem, told_sem,
):
    nx, ny, span, cin, cout, cap_x, cap_y, depth = dims
    half_x, half_y, half_z = cap_x // 2, cap_y // 2, depth // 2
    own = cout // ny
    planes = nx // span
    own = cout // ny
    half = planes // 2
    cells = half_x * half_z
    tall = patches.shape[1]
    window = band.shape[1] // 9
    reach = half_y // GROUP

    gx, gy = lax.axis_index("gx"), lax.axis_index("gy")
    iz, ix = gx // span, gx % span

    at_seam = (iz == half - 1) | (iz == half)
    across = jnp.where(iz == half, gx - span, gx + span)

    def wrap(value, size):
        return jnp.where(value >= size, value - size, value)

    order = [ny // 2]
    for step in range(1, ny // 2):
        order += [ny // 2 + step, ny // 2 - step]

    def x_peer(d):
        return (iz * span + wrap(ix + d, span), gy)

    def half_peer(d):
        return ((iz // half * half + wrap(iz % half + d, half)) * span + ix, gy)

    def z_peer(d):
        return (wrap(iz + d, planes) * span + ix, gy)

    barrier = pltpu.get_barrier_semaphore()

    def greet(device):
        pl.semaphore_signal(barrier, inc=1, device_id=device, device_id_type=MESH)

    for d in order:
        greet((gx, wrap(gy + d, ny)))
    above_us, below_us = gx > 0, gx < nx - 1

    @pl.when(above_us)
    def _():
        greet((gx - 1, gy))
        greet((gx - 1, wrap(gy + ny - 1, ny)))

    @pl.when(below_us)
    def _():
        greet((gx + 1, gy))
        greet((gx + 1, wrap(gy + 1, ny)))

    for d in range(1, span):
        greet(x_peer(d))
    for d in range(1, half):
        greet(half_peer(d))
    if half:
        @pl.when(at_seam)
        def _():
            greet((across, gy))

    load = pltpu.make_async_copy(fields_hbm, fields, load_sem.at[0])
    load.start()
    mine = pltpu.make_async_copy(
        grad_hbm.at[:, :, pl.ds(gy * half_y, half_y), :],
        grads.at[pl.ds(gy * own, own)],
        load_sem.at[1],
    )
    mine.start()
    small = [
        pltpu.make_async_copy(src, dst, load_sem.at[3 + i])
        for i, (src, dst) in enumerate(
            ((rows_hbm, rows_ref), (cols_hbm, cols_ref), (weight_hbm, weight_ref), (bias_hbm, bias_ref))
        )
    ]
    for copy in small:
        copy.start()
    guests = ny - 1 + span - 1
    guests = guests + jnp.where(above_us, 2, 0) + jnp.where(below_us, 2, 0)
    if half:
        guests = guests + half - 1 + jnp.where(at_seam, 1, 0)
    pl.semaphore_wait(barrier, guests)

    def halo_copy(index, src, dst, dx, dy):
        return pltpu.make_async_remote_copy(
            src_ref=src, dst_ref=dst, send_sem=halo_send.at[index], recv_sem=halo_recv.at[index],
            device_id=(gx + dx, wrap(gy + dy, ny)), device_id_type=MESH,
        )

    def grad_copy(d):
        to = wrap(gy + d, ny)
        return pltpu.make_async_remote_copy(
            src_ref=grad_hbm.at[:, :, pl.ds(to * half_y, half_y), :],
            dst_ref=grads.at[pl.ds(gy * own, own)],
            send_sem=grad_send.at[d], recv_sem=grad_recv.at[d],
            device_id=(gx, to), device_id_type=MESH,
        )

    rows_out = halo_copy(0, fields_hbm.at[:, cap_x - 1], above, 1, 0)

    @pl.when(below_us)
    def _():
        rows_out.start()

    for d in order[:FIRST]:
        grad_copy(d).start()

    load.wait()
    for x in range(cap_x):
        for c in range(cin):
            for h in range(2):
                lines[x + 1, h, pl.ds(cin + c, cap_y, stride=cin), :] = (
                    fields[c, x, :, h * half_z:(h + 1) * half_z].astype(F32)
                )
        for h in range(2):
            rows32[x * cin:(x + 1) * cin, h * half_z:(h + 1) * half_z] = (
                lines[x + 1, h, cin * cap_y:cin * (cap_y + 1), :]
            )
    side[...] = rows32[...].astype(BF16)
    side_out = halo_copy(1, side, side_in, 0, 1)
    side_out.start()
    corner_out = halo_copy(2, side, corner_in, 1, 1)

    @pl.when(below_us)
    def _():
        corner_out.start()

    for d in order[FIRST:]:
        grad_copy(d).start()

    if half:
        @pl.when(at_seam)
        def _():
            pl.semaphore_signal(seam_sem, inc=1, device_id=(across, gy), device_id_type=MESH)

    z_at = lax.broadcasted_iota(jnp.int32, (depth, 3 * half_z), 0)
    n_at = lax.broadcasted_iota(jnp.int32, (depth, 3 * half_z), 1)
    spread[...] = jnp.where(
        z_at == 2 * (n_at % half_z) - 1 + n_at // half_z, 1.0, 0.0
    ).astype(BF16)

    n_row = lax.broadcasted_iota(jnp.int32, (1, 9 * window), 1)
    off, place = n_row // window, n_row % window
    first_tap = (place % cin) * 27 + (off // 3) * 9 + off % 3
    ext_y = place // cin
    w_at = lax.broadcasted_iota(jnp.int32, (LANES, 9 * window), 0)
    for b in range(3):
        taps_b[b] = jnp.where(w_at == first_tap + 3 * b, 1.0, 0.0).astype(BF16)
    for copy in small:
        copy.wait()

    by_tap = [
        jnp.dot(weight_ref[...], taps_b[b, 0:cin * 27, :], preferred_element_type=F32)
        for b in range(3)
    ]
    for i in range(GROUP):
        value = jnp.zeros((cout, 9 * window), F32)
        for b in range(3):
            value = jnp.where(ext_y == 2 * i + b, by_tap[b], value)
        band[i * cout:(i + 1) * cout, :] = value.astype(BF16)

    side_out.wait_recv()

    @pl.when(above_us)
    def _():
        rows_out.wait_recv()
        corner_out.wait_recv()

    edge_x = cap_x - rows_ref[gx]
    edge_y = cap_y - cols_ref[gy]
    inner_x = gx > 0
    inner_y = gy > 0
    rows32[...] = side_in[...].astype(F32)
    corner = corner_in[cin * cap_x - 16:cin * cap_x, :].astype(F32)[16 - cin:16, :]
    for x in range(cap_x + 1):
        line = jnp.where((x == edge_x) & inner_x & inner_y, corner, 0.0)
        if x > 0:
            line = jnp.where((x > edge_x) & inner_y, rows32[(x - 1) * cin:x * cin, :], line)
        for i in range(8 // cin):
            border[x, i * cin:(i + 1) * cin, :] = line
    for c in range(cin):
        for h in range(2):
            lines[0, h, pl.ds(cin + c, cap_y, stride=cin), :] = (
                above[c, :, h * half_z:(h + 1) * half_z].astype(F32)
            )
    whole = (tall // 8, 8, half_z)
    y_at = (
        lax.broadcasted_iota(jnp.int32, whole, 0) * 8 + lax.broadcasted_iota(jnp.int32, whole, 1)
    ) // cin
    inside = (y_at > edge_y) & (y_at <= cap_y)
    at_edge = y_at == edge_y
    for x in range(cap_x + 1):
        halves = []
        for h in range(2):
            value = jnp.where((x == edge_x) & inner_x, lines[0, h], 0.0)
            if x > 0:
                value = jnp.where(x > edge_x, lines[x, h], value)
            line = border[x, :, h * half_z:(h + 1) * half_z][None]
            value = jnp.where(inside, value.reshape(whole), jnp.where(at_edge, line, 0.0))
            halves.append(value.reshape(tall, half_z).astype(BF16))
        value = jnp.concatenate(halves, axis=1)
        split = jnp.dot(
            value, spread[...], preferred_element_type=F32
        ).astype(BF16)
        for a in range(3):
            if (x - a) % 2 == 0 and 0 <= (x - a) // 2 < half_x:
                p = (x - a) // 2
                for k in range(3):
                    patches[a * 3 + k, :, p * half_z:(p + 1) * half_z] = (
                        split[:, k * half_z:(k + 1) * half_z]
                    )

    def windows(m):
        first = 2 * GROUP * cin * m
        return patches[:, first:first + window, :].reshape(9 * window, cells)

    for m in range(reach):
        value = jnp.dot(band[...], windows(m), preferred_element_type=F32)
        for i in range(GROUP):
            for p in range(half_x):
                acc[p, pl.ds(m * GROUP + i, cout, stride=half_y), :] = (
                    value[i * cout:(i + 1) * cout, p * half_z:(p + 1) * half_z]
                )
    q_live = 2 * lax.broadcasted_iota(jnp.int32, (half_y, half_z), 0) >= edge_y

    def stem_copy(d):
        to = wrap(gy + d, ny)
        return pltpu.make_async_remote_copy(
            src_ref=stage.at[pl.ds(to * own, own)],
            dst_ref=stem_hbm.at[:, :, pl.ds(gy * half_y, half_y), :],
            send_sem=stem_send.at[d], recv_sem=stem_recv.at[d],
            device_id=(gx, to), device_id_type=MESH,
        )

    def activate(o):
        rows = pl.ds(pl.multiple_of(o * half_y, half_y), half_y)
        for p in range(half_x):
            live = q_live & (2 * p >= edge_x)
            pre = jnp.where(live, acc[p, rows, :] + bias_ref[o], 0.0).astype(BF16).astype(F32)
            sigma = 1.0 / (1.0 + jnp.exp(-pre))
            stage[o, p] = (pre * sigma).astype(BF16)
            slope[p, rows, :] = jnp.where(live, sigma * (1.0 + pre * (1.0 - sigma)), 0.0)

    def forward(o, carry):
        activate(o)
        return carry

    lax.fori_loop(0, cout, forward, 0)
    keep = pltpu.make_async_copy(
        stage.at[pl.ds(gy * own, own)],
        stem_hbm.at[:, :, pl.ds(gy * half_y, half_y), :],
        load_sem.at[2],
    )
    keep.start()

    if half:
        @pl.when(at_seam)
        def _():
            pl.semaphore_wait(seam_sem, 1)
            for d in range(1, half):
                pl.semaphore_signal(
                    told_sem, inc=1, device_id=half_peer(d), device_id_type=MESH
                )

    sources = [wrap(gy + ny - d, ny) for d in order] + [gy]
    per = cout // 2

    def part_copy(slot):
        return pltpu.make_async_remote_copy(
            src_ref=part.at[slot], dst_ref=part_in.at[slot],
            send_sem=part_send.at[slot], recv_sem=part_recv.at[slot],
            device_id=(gx, sources[slot]), device_id_type=MESH,
        )

    def backward(group):
        slots = range(group * ny // 2, (group + 1) * ny // 2)
        for slot in slots:
            for i in range(own):
                o = sources[slot] * own + i
                rows = pl.ds(pl.multiple_of(o * half_y, half_y), half_y)
                at = (slot * own + i) * half_y
                for p in range(half_x):
                    value = (grads[o, p].astype(F32) * slope[p, rows, :]).astype(BF16)
                    grad_pre[p, at:at + half_y, :] = value.astype(F32)
        first = slots[0] * own * half_y
        corr = jnp.zeros((GROUP * per, 9 * window), F32)
        bias_sum = jnp.zeros((per, cells), F32)
        for m in range(reach):
            values = [
                jnp.concatenate(
                    [
                        grad_pre[p, pl.ds(first + m * GROUP + i, per, stride=half_y), :]
                        for p in range(half_x)
                    ],
                    axis=1,
                )
                for i in range(GROUP)
            ]
            bias_sum = bias_sum + sum(values[1:], values[0])
            corr = corr + nt_dot(jnp.concatenate(values, axis=0).astype(BF16), windows(m))
        total = jnp.zeros((per, LANES), F32)
        for b in range(3):
            picked = jnp.zeros((per, 9 * window), F32)
            for i in range(GROUP):
                picked = jnp.where(ext_y == 2 * i + b, corr[i * per:(i + 1) * per, :], picked)
            high = picked.astype(BF16)
            low = (picked - high.astype(F32)).astype(BF16)
            total = total + (nt_dot(high, taps_b[b]) + nt_dot(low, taps_b[b]))
        lane = lax.broadcasted_iota(jnp.int32, (per, LANES), 1)
        total = jnp.where(lane == cin * 27, jnp.sum(bias_sum, axis=1, keepdims=True), total)
        for slot in slots:
            at = (slot - slots[0]) * own
            part[slot] = total[at:at + own]
        for slot in slots:
            if slot < ny - 1:
                part_copy(slot).start()

    for d in order[:ny // 2]:
        grad_copy(d).wait_recv()
    for d in order[:CUTS[0]]:
        stem_copy(d).start()
    backward(0)
    mine.wait()
    for d in order[ny // 2:]:
        grad_copy(d).wait_recv()
    backward(1)
    for d in order[CUTS[0]:CUTS[1]]:
        stem_copy(d).start()
    held = part[ny - 1]
    for slot in range(ny - 1):
        part_copy(slot).wait_recv()
        held = held + part_in[slot]
    xpart[...] = held

    def x_copy(d):
        return pltpu.make_async_remote_copy(
            src_ref=xpart, dst_ref=xpart_in.at[ix],
            send_sem=x_send.at[d], recv_sem=x_recv.at[d],
            device_id=x_peer(d), device_id_type=MESH,
        )

    def z_copy(d):
        return pltpu.make_async_remote_copy(
            src_ref=zpart, dst_ref=zpart_in.at[iz],
            send_sem=z_send.at[d], recv_sem=z_recv.at[d],
            device_id=z_peer(d), device_id_type=MESH,
        )

    for d in range(1, span):
        x_copy(d).start()
    for d in order[CUTS[1]:CUTS[2]]:
        stem_copy(d).start()
    xpart_in[ix] = xpart[...]
    for d in range(1, span):
        x_copy(d).wait_recv()
    zpart[...] = sum([xpart_in[i] for i in range(1, span)], xpart_in[0])
    if half:
        @pl.when(jnp.logical_not(at_seam))
        def _():
            pl.semaphore_wait(told_sem, 1)

    for d in range(1, planes):
        z_copy(d).start()
    for d in order[CUTS[2]:]:
        stem_copy(d).start()
    zpart_in[iz] = zpart[...]
    for d in range(1, planes):
        z_copy(d).wait_recv()
    sums_ref[...] = sum([zpart_in[i] for i in range(1, planes)], zpart_in[0])

    for d in order:
        stem_copy(d).wait_recv()
        stem_copy(d).wait_send()
        grad_copy(d).wait_send()
    for slot in range(ny - 1):
        part_copy(slot).wait_send()
    for d in range(1, span):
        x_copy(d).wait_send()
    for d in range(1, planes):
        z_copy(d).wait_send()
    side_out.wait_send()

    @pl.when(below_us)
    def _():
        rows_out.wait_send()
        corner_out.wait_send()

    keep.wait()


def hand_over(own, taps, landed, sums, stem, weight_grad, bias_grad, scalars, sem):
    out = pltpu.make_async_copy(landed, stem, sem.at[0])
    out.start()
    read = pltpu.make_async_copy(sums, scalars, sem.at[1])
    read.start()
    weight_grad[...] = sums[0:own, 0:taps]
    read.wait()
    for i in range(own):
        bias_grad[i] = scalars[i, taps]
    out.wait()


def local(nx, ny, span, fields, rows_live, cols_live, weight, bias, grad_out):
    cin, cap_x, cap_y, depth = fields.shape
    cout = weight.shape[0]
    half_x, half_y, half_z = cap_x // 2, cap_y // 2, depth // 2
    planes = nx // span
    own = cout // ny
    cells = half_x * half_z
    tall = cin * (cap_y + 4)
    window = -(-(2 * GROUP + 1) * cin // 16) * 16
    dims = (nx, ny, span, cin, cout, cap_x, cap_y, depth)
    vmem = pl.BlockSpec(memory_space=pltpu.VMEM)
    hbm = pl.BlockSpec(memory_space=pl.ANY)
    dma = pltpu.SemaphoreType.DMA
    landed, sums = pl.pallas_call(
        functools.partial(kernel, dims),
        out_shape=(
            pltpu.VMEM(grad_out.shape, BF16),
            pltpu.VMEM((own, LANES), F32),
        ),
        in_specs=[hbm] * 6,
        out_specs=(vmem, vmem),
        scratch_shapes=[
            pltpu.SMEM(rows_live.shape, jnp.int32),
            pltpu.SMEM(cols_live.shape, jnp.int32),
            pltpu.VMEM(weight.shape, BF16),
            pltpu.SMEM(bias.shape, F32),
            pltpu.VMEM((cin, cap_x, cap_y, depth), BF16),
            pltpu.VMEM((cin, cap_y, depth), BF16),
            pltpu.VMEM((cin * cap_x, depth), BF16),
            pltpu.VMEM((cin * cap_x, depth), BF16),
            pltpu.VMEM((cin * cap_x, depth), BF16),
            pltpu.VMEM((cin * cap_x, depth), F32),
            pltpu.VMEM((cap_x + 1, 2, tall, half_z), F32),
            pltpu.VMEM((cap_x + 1, 8, depth), F32),
            pltpu.VMEM((depth, 3 * half_z), BF16),
            pltpu.VMEM((3, LANES, 9 * window), BF16),
            pltpu.VMEM((GROUP * cout, 9 * window), BF16),
            pltpu.VMEM((9, tall, cells), BF16),
            pltpu.VMEM((half_x, cout * half_y, half_z), F32),
            pltpu.VMEM((half_x, cout * half_y, half_z), F32),
            pltpu.VMEM((cout, half_x, half_y, half_z), BF16),
            pltpu.VMEM((cout, half_x, half_y, half_z), BF16),
            pltpu.VMEM((half_x, cout * half_y, half_z), F32),
            pltpu.VMEM((ny, own, LANES), F32),
            pltpu.VMEM((ny, own, LANES), F32),
            pltpu.VMEM((own, LANES), F32),
            pltpu.VMEM((span, own, LANES), F32),
            pltpu.VMEM((own, LANES), F32),
            pltpu.VMEM((planes, own, LANES), F32),
            dma((7,)), dma((3,)), dma((3,)),
            dma((ny,)), dma((ny,)), dma((ny,)), dma((ny,)), dma((ny,)), dma((ny,)),
            dma((span,)), dma((span,)), dma((planes,)), dma((planes,)),
            pltpu.SemaphoreType.REGULAR, pltpu.SemaphoreType.REGULAR,
        ],
        compiler_params=pltpu.CompilerParams(
            collective_id=0, has_side_effects=True, vmem_limit_bytes=63 * 1024 * 1024
        ),
    )(fields, rows_live, cols_live, weight, bias, grad_out)
    taps = weight.shape[1]
    return pl.pallas_call(
        functools.partial(hand_over, own, taps),
        out_shape=(
            jax.ShapeDtypeStruct(grad_out.shape, BF16),
            jax.ShapeDtypeStruct((own, taps), F32),
            jax.ShapeDtypeStruct((own,), F32),
        ),
        in_specs=[vmem, vmem],
        out_specs=(hbm, vmem, pl.BlockSpec(memory_space=pltpu.SMEM)),
        scratch_shapes=[pltpu.SMEM((own, LANES), F32), dma((2,))],
        compiler_params=pltpu.CompilerParams(vmem_limit_bytes=4 * 1024 * 1024),
    )(landed, sums)


def solution(mesh):
    nx, ny = mesh.shape["gx"], mesh.shape["gy"]
    span = 4 if nx % 4 == 0 else 1
    in_specs = (P(None, "gx", "gy", None), P(), P(), P(), P(), P("gy", "gx", None, None))
    out_specs = (P("gy", "gx", None, None), P("gy", None), P("gy"))
    run = functools.partial(local, nx, ny, span)
    return jax.shard_map(run, mesh=mesh, in_specs=in_specs, out_specs=out_specs, check_vma=False)
```

```python
import functools

import jax
import jax.numpy as jnp
from jax import lax
from jax.experimental import pallas as pl
from jax.experimental.pallas import tpu as pltpu
from jax.sharding import PartitionSpec as P

MESH = pl.DeviceIdType.MESH
F32 = jnp.float32
BF16 = jnp.bfloat16
LANES = 128
CUTS = (1, 3, 8)
FIRST = 2
GROUP = 4


def nt_dot(a, b):
    return lax.dot_general(a, b, (((1,), (1,)), ((), ())), preferred_element_type=F32)


def kernel(
    dims,
    fields_hbm, rows_hbm, cols_hbm, weight_hbm, bias_hbm, grad_hbm,
    stem_hbm, sums_ref,
    rows_ref, cols_ref, weight_ref, bias_ref, fields, above, side, side_in, corner_in,
    rows32, lines, border, spread, taps_b, band, patches, acc, slope, stage, grads, grad_pre,
    part, part_in, xpart, xpart_in, zpart, zpart_in,
    load_sem, halo_send, halo_recv, grad_send, grad_recv, stem_send, stem_recv,
    part_send, part_recv, x_send, x_recv, z_send, z_recv, seam_sem, told_sem,
):
    nx, ny, span, cin, cout, cap_x, cap_y, depth = dims
    half_x, half_y, half_z = cap_x // 2, cap_y // 2, depth // 2
    own = cout // ny
    planes = nx // span
    own = cout // ny
    half = planes // 2
    cells = half_x * half_z
    tall = patches.shape[1]
    window = band.shape[1] // 9
    reach = half_y // GROUP

    gx, gy = lax.axis_index("gx"), lax.axis_index("gy")
    iz, ix = gx // span, gx % span

    at_seam = (iz == half - 1) | (iz == half)
    across = jnp.where(iz == half, gx - span, gx + span)

    def wrap(value, size):
        return jnp.where(value >= size, value - size, value)

    order = [ny // 2]
    for step in range(1, ny // 2):
        order += [ny // 2 + step, ny // 2 - step]

    def x_peer(d):
        return (iz * span + wrap(ix + d, span), gy)

    def half_peer(d):
        return ((iz // half * half + wrap(iz % half + d, half)) * span + ix, gy)

    def z_peer(d):
        return (wrap(iz + d, planes) * span + ix, gy)

    barrier = pltpu.get_barrier_semaphore()

    def greet(device):
        pl.semaphore_signal(barrier, inc=1, device_id=device, device_id_type=MESH)

    for d in order:
        greet((gx, wrap(gy + d, ny)))
    above_us, below_us = gx > 0, gx < nx - 1

    @pl.when(above_us)
    def _():
        greet((gx - 1, gy))
        greet((gx - 1, wrap(gy + ny - 1, ny)))

    @pl.when(below_us)
    def _():
        greet((gx + 1, gy))
        greet((gx + 1, wrap(gy + 1, ny)))

    for d in range(1, span):
        greet(x_peer(d))
    for d in range(1, half):
        greet(half_peer(d))
    if half:
        @pl.when(at_seam)
        def _():
            greet((across, gy))

    load = pltpu.make_async_copy(fields_hbm, fields, load_sem.at[0])
    load.start()
    mine = pltpu.make_async_copy(
        grad_hbm.at[:, :, pl.ds(gy * half_y, half_y), :],
        grads.at[pl.ds(gy * own, own)],
        load_sem.at[1],
    )
    mine.start()
    small = [
        pltpu.make_async_copy(src, dst, load_sem.at[3 + i])
        for i, (src, dst) in enumerate(
            ((rows_hbm, rows_ref), (cols_hbm, cols_ref), (weight_hbm, weight_ref), (bias_hbm, bias_ref))
        )
    ]
    for copy in small:
        copy.start()
    guests = ny - 1 + span - 1
    guests = guests + jnp.where(above_us, 2, 0) + jnp.where(below_us, 2, 0)
    if half:
        guests = guests + half - 1 + jnp.where(at_seam, 1, 0)
    pl.semaphore_wait(barrier, guests)

    def halo_copy(index, src, dst, dx, dy):
        return pltpu.make_async_remote_copy(
            src_ref=src, dst_ref=dst, send_sem=halo_send.at[index], recv_sem=halo_recv.at[index],
            device_id=(gx + dx, wrap(gy + dy, ny)), device_id_type=MESH,
        )

    def grad_copy(d):
        to = wrap(gy + d, ny)
        return pltpu.make_async_remote_copy(
            src_ref=grad_hbm.at[:, :, pl.ds(to * half_y, half_y), :],
            dst_ref=grads.at[pl.ds(gy * own, own)],
            send_sem=grad_send.at[d], recv_sem=grad_recv.at[d],
            device_id=(gx, to), device_id_type=MESH,
        )

    rows_out = halo_copy(0, fields_hbm.at[:, cap_x - 1], above, 1, 0)

    @pl.when(below_us)
    def _():
        rows_out.start()

    for d in order[:FIRST]:
        grad_copy(d).start()

    load.wait()
    for x in range(cap_x):
        for c in range(cin):
            for h in range(2):
                lines[x + 1, h, pl.ds(cin + c, cap_y, stride=cin), :] = (
                    fields[c, x, :, h * half_z:(h + 1) * half_z].astype(F32)
                )
        for h in range(2):
            rows32[x * cin:(x + 1) * cin, h * half_z:(h + 1) * half_z] = (
                lines[x + 1, h, cin * cap_y:cin * (cap_y + 1), :]
            )
    side[...] = rows32[...].astype(BF16)
    side_out = halo_copy(1, side, side_in, 0, 1)
    side_out.start()
    corner_out = halo_copy(2, side, corner_in, 1, 1)

    @pl.when(below_us)
    def _():
        corner_out.start()

    for d in order[FIRST:]:
        grad_copy(d).start()

    if half:
        @pl.when(at_seam)
        def _():
            pl.semaphore_signal(seam_sem, inc=1, device_id=(across, gy), device_id_type=MESH)

    z_at = lax.broadcasted_iota(jnp.int32, (depth, 3 * half_z), 0)
    n_at = lax.broadcasted_iota(jnp.int32, (depth, 3 * half_z), 1)
    spread[...] = jnp.where(
        z_at == 2 * (n_at % half_z) - 1 + n_at // half_z, 1.0, 0.0
    ).astype(BF16)

    n_row = lax.broadcasted_iota(jnp.int32, (1, 9 * window), 1)
    off, place = n_row // window, n_row % window
    first_tap = (place % cin) * 27 + (off // 3) * 9 + off % 3
    ext_y = place // cin
    w_at = lax.broadcasted_iota(jnp.int32, (LANES, 9 * window), 0)
    for b in range(3):
        taps_b[b] = jnp.where(w_at == first_tap + 3 * b, 1.0, 0.0).astype(BF16)
    for copy in small:
        copy.wait()

    by_tap = [
        jnp.dot(weight_ref[...], taps_b[b, 0:cin * 27, :], preferred_element_type=F32)
        for b in range(3)
    ]
    for i in range(GROUP):
        value = jnp.zeros((cout, 9 * window), F32)
        for b in range(3):
            value = jnp.where(ext_y == 2 * i + b, by_tap[b], value)
        band[i * cout:(i + 1) * cout, :] = value.astype(BF16)

    side_out.wait_recv()

    @pl.when(above_us)
    def _():
        rows_out.wait_recv()
        corner_out.wait_recv()

    edge_x = cap_x - rows_ref[gx]
    edge_y = cap_y - cols_ref[gy]
    inner_x = gx > 0
    inner_y = gy > 0
    rows32[...] = side_in[...].astype(F32)
    corner = corner_in[cin * cap_x - 16:cin * cap_x, :].astype(F32)[16 - cin:16, :]
    for x in range(cap_x + 1):
        line = jnp.where((x == edge_x) & inner_x & inner_y, corner, 0.0)
        if x > 0:
            line = jnp.where((x > edge_x) & inner_y, rows32[(x - 1) * cin:x * cin, :], line)
        for i in range(8 // cin):
            border[x, i * cin:(i + 1) * cin, :] = line
    for c in range(cin):
        for h in range(2):
            lines[0, h, pl.ds(cin + c, cap_y, stride=cin), :] = (
                above[c, :, h * half_z:(h + 1) * half_z].astype(F32)
            )
    whole = (tall // 8, 8, half_z)
    y_at = (
        lax.broadcasted_iota(jnp.int32, whole, 0) * 8 + lax.broadcasted_iota(jnp.int32, whole, 1)
    ) // cin
    inside = (y_at > edge_y) & (y_at <= cap_y)
    at_edge = y_at == edge_y
    for x in range(cap_x + 1):
        halves = []
        for h in range(2):
            value = jnp.where((x == edge_x) & inner_x, lines[0, h], 0.0)
            if x > 0:
                value = jnp.where(x > edge_x, lines[x, h], value)
            line = border[x, :, h * half_z:(h + 1) * half_z][None]
            value = jnp.where(inside, value.reshape(whole), jnp.where(at_edge, line, 0.0))
            halves.append(value.reshape(tall, half_z).astype(BF16))
        value = jnp.concatenate(halves, axis=1)
        split = jnp.dot(
            value, spread[...], preferred_element_type=F32
        ).astype(BF16)
        for a in range(3):
            if (x - a) % 2 == 0 and 0 <= (x - a) // 2 < half_x:
                p = (x - a) // 2
                for k in range(3):
                    patches[a * 3 + k, :, p * half_z:(p + 1) * half_z] = (
                        split[:, k * half_z:(k + 1) * half_z]
                    )

    def windows(m):
        first = 2 * GROUP * cin * m
        return patches[:, first:first + window, :].reshape(9 * window, cells)

    for m in range(reach):
        value = jnp.dot(band[...], windows(m), preferred_element_type=F32)
        for i in range(GROUP):
            for p in range(half_x):
                acc[p, pl.ds(m * GROUP + i, cout, stride=half_y), :] = (
                    value[i * cout:(i + 1) * cout, p * half_z:(p + 1) * half_z]
                )
    q_live = 2 * lax.broadcasted_iota(jnp.int32, (half_y, half_z), 0) >= edge_y

    def stem_copy(d):
        to = wrap(gy + d, ny)
        return pltpu.make_async_remote_copy(
            src_ref=stage.at[pl.ds(to * own, own)],
            dst_ref=stem_hbm.at[:, :, pl.ds(gy * half_y, half_y), :],
            send_sem=stem_send.at[d], recv_sem=stem_recv.at[d],
            device_id=(gx, to), device_id_type=MESH,
        )

    def activate(o):
        rows = pl.ds(pl.multiple_of(o * half_y, half_y), half_y)
        for p in range(half_x):
            live = q_live & (2 * p >= edge_x)
            pre = jnp.where(live, acc[p, rows, :] + bias_ref[o], 0.0).astype(BF16).astype(F32)
            sigma = 1.0 / (1.0 + jnp.exp(-pre))
            stage[o, p] = (pre * sigma).astype(BF16)
            slope[p, rows, :] = jnp.where(live, sigma * (1.0 + pre * (1.0 - sigma)), 0.0)

    def forward(o, carry):
        activate(o)
        return carry

    lax.fori_loop(0, cout, forward, 0)
    keep = pltpu.make_async_copy(
        stage.at[pl.ds(gy * own, own)],
        stem_hbm.at[:, :, pl.ds(gy * half_y, half_y), :],
        load_sem.at[2],
    )
    keep.start()

    if half:
        @pl.when(at_seam)
        def _():
            pl.semaphore_wait(seam_sem, 1)
            for d in range(1, half):
                pl.semaphore_signal(
                    told_sem, inc=1, device_id=half_peer(d), device_id_type=MESH
                )

    sources = [wrap(gy + ny - d, ny) for d in order] + [gy]
    per = cout // 2

    def part_copy(slot):
        return pltpu.make_async_remote_copy(
            src_ref=part.at[slot], dst_ref=part_in.at[slot],
            send_sem=part_send.at[slot], recv_sem=part_recv.at[slot],
            device_id=(gx, sources[slot]), device_id_type=MESH,
        )

    def backward(group):
        slots = range(group * ny // 2, (group + 1) * ny // 2)
        for slot in slots:
            for i in range(own):
                o = sources[slot] * own + i
                rows = pl.ds(pl.multiple_of(o * half_y, half_y), half_y)
                at = (slot * own + i) * half_y
                for p in range(half_x):
                    value = (grads[o, p].astype(F32) * slope[p, rows, :]).astype(BF16)
                    grad_pre[p, at:at + half_y, :] = value.astype(F32)
        first = slots[0] * own * half_y
        corr = jnp.zeros((GROUP * per, 9 * window), F32)
        bias_sum = jnp.zeros((per, cells), F32)
        for m in range(reach):
            values = [
                jnp.concatenate(
                    [
                        grad_pre[p, pl.ds(first + m * GROUP + i, per, stride=half_y), :]
                        for p in range(half_x)
                    ],
                    axis=1,
                )
                for i in range(GROUP)
            ]
            bias_sum = bias_sum + sum(values[1:], values[0])
            corr = corr + nt_dot(jnp.concatenate(values, axis=0).astype(BF16), windows(m))
        total = jnp.zeros((per, LANES), F32)
        for b in range(3):
            picked = jnp.zeros((per, 9 * window), F32)
            for i in range(GROUP):
                picked = jnp.where(ext_y == 2 * i + b, corr[i * per:(i + 1) * per, :], picked)
            high = picked.astype(BF16)
            low = (picked - high.astype(F32)).astype(BF16)
            total = total + (nt_dot(high, taps_b[b]) + nt_dot(low, taps_b[b]))
        lane = lax.broadcasted_iota(jnp.int32, (per, LANES), 1)
        total = jnp.where(lane == cin * 27, jnp.sum(bias_sum, axis=1, keepdims=True), total)
        for slot in slots:
            at = (slot - slots[0]) * own
            part[slot] = total[at:at + own]
        for slot in slots:
            if slot < ny - 1:
                part_copy(slot).start()

    for d in order[:ny // 2]:
        grad_copy(d).wait_recv()
    for d in order[:CUTS[0]]:
        stem_copy(d).start()
    backward(0)
    mine.wait()
    for d in order[ny // 2:]:
        grad_copy(d).wait_recv()
    backward(1)
    for d in order[CUTS[0]:CUTS[1]]:
        stem_copy(d).start()
    held = part[ny - 1]
    for slot in range(ny - 1):
        part_copy(slot).wait_recv()
        held = held + part_in[slot]
    xpart[...] = held

    def x_copy(d):
        return pltpu.make_async_remote_copy(
            src_ref=xpart, dst_ref=xpart_in.at[ix],
            send_sem=x_send.at[d], recv_sem=x_recv.at[d],
            device_id=x_peer(d), device_id_type=MESH,
        )

    def z_copy(d):
        return pltpu.make_async_remote_copy(
            src_ref=zpart, dst_ref=zpart_in.at[iz],
            send_sem=z_send.at[d], recv_sem=z_recv.at[d],
            device_id=z_peer(d), device_id_type=MESH,
        )

    for d in range(1, span):
        x_copy(d).start()
    for d in order[CUTS[1]:CUTS[2]]:
        stem_copy(d).start()
    xpart_in[ix] = xpart[...]
    for d in range(1, span):
        x_copy(d).wait_recv()
    zpart[...] = sum([xpart_in[i] for i in range(1, span)], xpart_in[0])
    if half:
        @pl.when(jnp.logical_not(at_seam))
        def _():
            pl.semaphore_wait(told_sem, 1)

    for d in range(1, planes):
        z_copy(d).start()
    for d in order[CUTS[2]:]:
        stem_copy(d).start()
    zpart_in[iz] = zpart[...]
    for d in range(1, planes):
        z_copy(d).wait_recv()
    sums_ref[...] = sum([zpart_in[i] for i in range(1, planes)], zpart_in[0])

    for d in order:
        stem_copy(d).wait_recv()
        stem_copy(d).wait_send()
        grad_copy(d).wait_send()
    for slot in range(ny - 1):
        part_copy(slot).wait_send()
    for d in range(1, span):
        x_copy(d).wait_send()
    for d in range(1, planes):
        z_copy(d).wait_send()
    side_out.wait_send()

    @pl.when(below_us)
    def _():
        rows_out.wait_send()
        corner_out.wait_send()

    keep.wait()


def hand_over(own, taps, landed, sums, stem, weight_grad, bias_grad, scalars, sem):
    out = pltpu.make_async_copy(landed, stem, sem.at[0])
    out.start()
    read = pltpu.make_async_copy(sums, scalars, sem.at[1])
    read.start()
    weight_grad[...] = sums[0:own, 0:taps]
    read.wait()
    for i in range(own):
        bias_grad[i] = scalars[i, taps]
    out.wait()


def local(nx, ny, span, fields, rows_live, cols_live, weight, bias, grad_out):
    cin, cap_x, cap_y, depth = fields.shape
    cout = weight.shape[0]
    half_x, half_y, half_z = cap_x // 2, cap_y // 2, depth // 2
    planes = nx // span
    own = cout // ny
    cells = half_x * half_z
    tall = cin * (cap_y + 4)
    window = -(-(2 * GROUP + 1) * cin // 16) * 16
    dims = (nx, ny, span, cin, cout, cap_x, cap_y, depth)
    vmem = pl.BlockSpec(memory_space=pltpu.VMEM)
    hbm = pl.BlockSpec(memory_space=pl.ANY)
    dma = pltpu.SemaphoreType.DMA
    landed, sums = pl.pallas_call(
        functools.partial(kernel, dims),
        out_shape=(
            pltpu.VMEM(grad_out.shape, BF16),
            pltpu.VMEM((own, LANES), F32),
        ),
        in_specs=[hbm] * 6,
        out_specs=(vmem, vmem),
        scratch_shapes=[
            pltpu.SMEM(rows_live.shape, jnp.int32),
            pltpu.SMEM(cols_live.shape, jnp.int32),
            pltpu.VMEM(weight.shape, BF16),
            pltpu.SMEM(bias.shape, F32),
            pltpu.VMEM((cin, cap_x, cap_y, depth), BF16),
            pltpu.VMEM((cin, cap_y, depth), BF16),
            pltpu.VMEM((cin * cap_x, depth), BF16),
            pltpu.VMEM((cin * cap_x, depth), BF16),
            pltpu.VMEM((cin * cap_x, depth), BF16),
            pltpu.VMEM((cin * cap_x, depth), F32),
            pltpu.VMEM((cap_x + 1, 2, tall, half_z), F32),
            pltpu.VMEM((cap_x + 1, 8, depth), F32),
            pltpu.VMEM((depth, 3 * half_z), BF16),
            pltpu.VMEM((3, LANES, 9 * window), BF16),
            pltpu.VMEM((GROUP * cout, 9 * window), BF16),
            pltpu.VMEM((9, tall, cells), BF16),
            pltpu.VMEM((half_x, cout * half_y, half_z), F32),
            pltpu.VMEM((half_x, cout * half_y, half_z), F32),
            pltpu.VMEM((cout, half_x, half_y, half_z), BF16),
            pltpu.VMEM((cout, half_x, half_y, half_z), BF16),
            pltpu.VMEM((half_x, cout * half_y, half_z), F32),
            pltpu.VMEM((ny, own, LANES), F32),
            pltpu.VMEM((ny, own, LANES), F32),
            pltpu.VMEM((own, LANES), F32),
            pltpu.VMEM((span, own, LANES), F32),
            pltpu.VMEM((own, LANES), F32),
            pltpu.VMEM((planes, own, LANES), F32),
            dma((7,)), dma((3,)), dma((3,)),
            dma((ny,)), dma((ny,)), dma((ny,)), dma((ny,)), dma((ny,)), dma((ny,)),
            dma((span,)), dma((span,)), dma((planes,)), dma((planes,)),
            pltpu.SemaphoreType.REGULAR, pltpu.SemaphoreType.REGULAR,
        ],
        compiler_params=pltpu.CompilerParams(
            collective_id=0, has_side_effects=True, vmem_limit_bytes=63 * 1024 * 1024
        ),
    )(fields, rows_live, cols_live, weight, bias, grad_out)
    taps = weight.shape[1]
    return pl.pallas_call(
        functools.partial(hand_over, own, taps),
        out_shape=(
            jax.ShapeDtypeStruct(grad_out.shape, BF16),
            jax.ShapeDtypeStruct((own, taps), F32),
            jax.ShapeDtypeStruct((own,), F32),
        ),
        in_specs=[vmem, vmem],
        out_specs=(hbm, vmem, pl.BlockSpec(memory_space=pltpu.SMEM)),
        scratch_shapes=[pltpu.SMEM((own, LANES), F32), dma((2,))],
        compiler_params=pltpu.CompilerParams(vmem_limit_bytes=4 * 1024 * 1024),
    )(landed, sums)


def solution(mesh):
    nx, ny = mesh.shape["gx"], mesh.shape["gy"]
    span = 4 if nx % 4 == 0 else 1
    in_specs = (P(None, "gx", "gy", None), P(), P(), P(), P(), P("gy", "gx", None, None))
    out_specs = (P("gy", "gx", None, None), P("gy", None), P("gy"))
    run = functools.partial(local, nx, ny, span)
    return jax.shard_map(run, mesh=mesh, in_specs=in_specs, out_specs=out_specs, check_vma=False)
```
